128 devices in a mesh: aa: 16 (over y, x), ba: 8 (over z, core).
Axes of the slice: x: 4, y: 4, z: 4, core: 2. Of those that a mesh axis runs over, the one named last changes fastest.
Arguments:
- bricks: bfloat16 [16384, 4096], P(('aa', 'ba')), may hold values from -6 to 6
- transfer: float32 [2, 4], replicated, may hold values from -1.5 to 1.5
- assignment: int32 [16384, 1], replicated, may hold values from 0 to 127; in each aligned block of 128 rows (0 to 127, 128 to 255, ...) at most 2 rows name the same one
- brick_cell: int32 [16384], replicated, may hold values from 0 to 16383, each once
- depth_rank: int32 [2, 16384], replicated, may hold values from 0 to 16383, each once within a row
Outputs:
- frame_z: float32 [4, 128, 2048], P(None, 'ba', 'aa')
- frame_x: float32 [4, 128, 2048], P(None, 'ba', 'aa')
The draws below stay inside these ranges and needn't reach their ends.
Inputs may be any that keep to these rules, and one draw needn't show every extreme that they name: `assignment`: within each aligned block of 128 rows (the bricks stored on one device) no renderer is named by more than 2 rows; every renderer is named by some row. `brick_cell`: each grid cell holds exactly one brick. `depth_rank`: each row names every brick once.
All inputs are finite; a program needn't handle non-finite values.
Results may differ from the reference program's by a relative error of at most 0.0003.
Values may be sent and summed in bfloat16 or wider, within the bound.
No kernel may reach another device: no remote copies, remote signals or barrier semaphores. Data moves between devices by JAX's collectives and lax.ppermute only.
A program may use at most 128 MiB of HBM per device.

```python
import math
import jax
import jax.numpy as jnp
import numpy as np
from jax import lax

SIDE = 1024
EDGE = 16
BRICK_DEV = 128
BRICKS = 16384
CAP = 2
DEVICES = 128


def shard_levels(own_key, extent, cuts, smallest, top_value):
    factor_of, own = 1.0, jax.random.fold_in(own_key, 6)
    for axis_at, parts in cuts:
        heights = jnp.exp(jax.random.uniform(jax.random.fold_in(own, axis_at), (parts,), jnp.float32, smallest / len(cuts), top_value / len(cuts)))
        factor_of = factor_of * jnp.repeat(heights, extent[axis_at] // parts).reshape([-1 if axis == axis_at else 1 for axis in range(len(extent))])
    return factor_of


def assign_block(stream_key, own, number, rows, number_of, top, bound, lean):
    order = jax.random.permutation(stream_key, number_of)
    crowded, usual = shares(number_of, rows * top, bound, lean, True), shares(number_of, rows * top, bound, lean, False)
    places = jnp.arange(number_of)

    def named(sizes, rotation):
        used = int((sizes > 0).sum())
        fixed = max(1, used // 4)
        moved = fixed + (places - fixed + rotation * (used - fixed)) % max(1, number_of - fixed)
        return jnp.zeros((number_of,), jnp.int32).at[order[jnp.where(places < fixed, places, moved)]].set(jnp.asarray(sizes, jnp.int32))

    sizes = jnp.where(number % 4 == 0, named(crowded, number // 4), named(usual, number - number // 4 - 1))
    mixed = jax.random.permutation(jax.random.fold_in(own, 3), number_of)
    donor, receiver = mixed[0:number_of // 2 * 2:2], mixed[1:number_of // 2 * 2:2]
    slack = jnp.minimum(sizes[donor] - 1, bound - sizes[receiver]) // 2
    slack = jnp.where((donor == order[0]) | (receiver == order[0]) | (sizes[receiver] == 0), 0, jnp.maximum(slack, 0))
    moved = jax.random.randint(jax.random.fold_in(own, 4), (number_of // 2,), 0, 1 << 20) % (slack + 1)
    sizes = sizes.at[donor].add(-moved).at[receiver].add(moved)
    items = jnp.searchsorted(jnp.cumsum(sizes), jnp.arange(rows * top), side="right").astype(jnp.int32)
    listing = items.reshape(top, rows).T
    listing = listing[jax.random.permutation(jax.random.fold_in(own, 1), rows)]
    rotation = jax.random.randint(jax.random.fold_in(own, 2), (rows, 1), 0, top)
    return jnp.take_along_axis(listing, (jnp.arange(top)[None, :] + rotation) % top, axis=1)


def shares(number_of, total, limit, slope, full):
    loads = [(1 << 20) // math.isqrt(rank ** slope) + 1 for rank in range(1, number_of + 1)]
    largest = limit if full else min(limit, max(-(-total // number_of), total * loads[0] // sum(loads)))
    least = 1 if total - largest >= number_of - 1 else 0
    counts, spare = [largest] + [least] * (number_of - 1), total - largest - least * (number_of - 1)
    while spare > 0:
        candidates = [i for i in range(1, number_of) if counts[i] < largest] or [i for i in range(1, number_of) if counts[i] < limit]
        whole, left = sum([loads[i] for i in candidates]), spare
        for i in candidates:
            extra = min(limit - counts[i], max(1, left * loads[i] // whole), spare)
            counts[i] = counts[i] + extra
            spare = spare - extra
    return np.array(counts)


def bell_draw(key, dims, scale, bound, split=(), dtype=jnp.bfloat16):
    gain = shard_levels(key, dims, split, -0.22, 0.18) if split else 1.0
    result = jax.random.normal(key, dims, jnp.float32) * scale * gain
    return jnp.minimum(jnp.maximum(result, -bound), bound).astype(dtype)


def setup_inputs(seed: int = 0) -> dict:
    splits = jax.random.split(jax.random.key(seed), 6)
    bricks = bell_draw(splits[0], (BRICKS, EDGE**3), 1.0, 6.0, ((0, 128),))
    transfer = jnp.clip(jax.random.uniform(splits[1], (2, 4), jnp.float32, -1.5, 1.5), -1.5, 1.5)
    assignment_keys = jax.random.split(jax.random.fold_in(splits[2], 1), BRICKS // BRICK_DEV)
    assignment_turns = jax.random.permutation(jax.random.fold_in(splits[2], 3), BRICKS // BRICK_DEV)
    assignment = jax.vmap(lambda own, number: assign_block(jax.random.fold_in(splits[2], 2), own, number, BRICK_DEV, DEVICES, 1, CAP, 2))(assignment_keys, assignment_turns).reshape((BRICKS, 1))
    brick_cell = jax.random.permutation(splits[3], BRICKS).astype(jnp.int32)
    depth_rank = jax.vmap(lambda own: jax.random.permutation(own, BRICKS))(jax.random.split(splits[4], 2)).reshape((2, BRICKS)).astype(jnp.int32)
    return {"bricks": bricks, "transfer": transfer, "assignment": assignment, "brick_cell": brick_cell, "depth_rank": depth_rank}


def upsample_matrix(brick_edge):
    row_ids = jnp.arange(2 * brick_edge)[:, None]
    col_ids = jnp.arange(brick_edge)[None, :]
    centre = row_ids // 2
    beside = jnp.clip(jnp.where(row_ids % 2 == 0, centre - 1, centre + 1), 0, brick_edge - 1)
    return 0.75 * (col_ids == centre).astype(jnp.float32) + 0.25 * (col_ids == beside).astype(jnp.float32)


def classify(samples, transfer):
    slopes = transfer[0]
    offsets = transfer[1]
    density = 2.0 * jax.nn.softplus(slopes[0] * samples + offsets[0]) / SIDE
    colours = [jax.nn.sigmoid(slopes[channel] * samples + offsets[channel]) for channel in (1, 2, 3)]
    return density, colours


def march_slices(density, colours):
    before = jnp.cumsum(density, axis=1) - density
    weight = -jnp.expm1(-density) * jnp.exp(-before)
    pieces = [jnp.sum(colour * weight, axis=1) for colour in colours] + [jnp.sum(density, axis=1)]
    return jnp.stack(pieces, axis=1)


def render_block(cells, transfer):
    number = cells.shape[0]
    matrix = upsample_matrix(EDGE)
    volume = cells.astype(jnp.float32).reshape(number, EDGE, EDGE, EDGE)
    samples = jnp.einsum('ax,by,cz,nxyz->nabc', matrix, matrix, matrix, volume, precision=lax.Precision.HIGHEST)
    density, colours = classify(samples, transfer)
    tile_side = 2 * EDGE

    def along_z(values):
        return jnp.transpose(values, (0, 3, 2, 1)).reshape(number, tile_side, tile_side * tile_side)

    def along_x(values):
        return values.reshape(number, tile_side, tile_side * tile_side)

    tiles_z = march_slices(along_z(density), [along_z(colour) for colour in colours])
    tiles_x = march_slices(along_x(density), [along_x(colour) for colour in colours])
    return tiles_z, tiles_x


def compose_frame(tile_data, footprint, renderer, ranks):
    across = SIDE // EDGE
    layers = BRICKS // (across * across)
    tile_side = 2 * EDGE
    ordering = jnp.lexsort((ranks, renderer, footprint)).astype(jnp.int32)
    sorted_tiles = tile_data[ordering].reshape(layers * across, across, 4, tile_side * tile_side)
    optical = sorted_tiles[:, :, 3]
    before = jnp.cumsum(optical, axis=1) - optical
    colour = jnp.sum(sorted_tiles[:, :, :3] * jnp.exp(-before)[:, :, None], axis=1)
    opacity = -jnp.expm1(-jnp.sum(optical, axis=1))
    picture = jnp.concatenate([colour, opacity[:, None]], axis=1)
    picture = picture.reshape(layers, across, 4, tile_side, tile_side).transpose(2, 0, 3, 1, 4)
    return picture.reshape(4, layers * tile_side, across * tile_side)


def reference(bricks, transfer, assignment, brick_cell, depth_rank):
    group_size = math.gcd(BRICKS, 256)
    blocks = bricks.reshape(BRICKS // group_size, group_size, EDGE ** 3)
    tiles_z, tiles_x = lax.map(lambda members: render_block(members, transfer), blocks)
    tiles_z = tiles_z.reshape(BRICKS, 4, -1)
    tiles_x = tiles_x.reshape(BRICKS, 4, -1)
    across = SIDE // EDGE
    grid_x = brick_cell % across
    grid_z = (brick_cell // across) % across
    grid_y = brick_cell // (across * across)
    renderer = assignment[:, 0]
    frame_z = compose_frame(tiles_z, grid_y * across + grid_x, renderer, depth_rank[0])
    frame_x = compose_frame(tiles_x, grid_y * across + grid_z, renderer, depth_rank[1])
    return frame_z, frame_x
```

```python
import functools

import jax
import jax.numpy as jnp
import numpy as np
from jax import lax
from jax.experimental import pallas as pl
from jax.experimental.pallas import tpu as pltpu
from jax.sharding import Mesh
from jax.sharding import PartitionSpec as P

SIDE = 1024
EDGE = 16
CAP = 16
CHIPS = 64
LOCAL = 256
HALF = EDGE * EDGE * EDGE // 2
F32 = jnp.float32
BF16 = jnp.bfloat16
I32 = jnp.int32
LOG2E = 1.4426950408889634
KAPPA = 2.0 * 0.6931471805599453 / SIDE
PLANE = ("y", "x")
CHIP = ("y", "x", "z")


def iota(shape, axis):
    return lax.broadcasted_iota(I32, shape, axis)


def ones_where(mask):
    return jnp.where(mask, 1.0, 0.0).astype(BF16)


def nt_dot(left, right):
    return lax.dot_general(left, right, (((1,), (1,)), ((), ())), preferred_element_type=F32)


def nn_dot(left, right):
    return jnp.dot(left, right, preferred_element_type=F32)


def parts_of(values, count):
    pieces = []
    rest = values
    for _ in range(count - 1):
        piece = rest.astype(BF16)
        pieces.append(piece)
        rest = rest - piece.astype(F32)
    return pieces + [rest.astype(BF16)]


def params(mib=48, semantics=None):
    return pltpu.CompilerParams(vmem_limit_bytes=mib * 1024 * 1024, dimension_semantics=semantics)


def upsample_np():
    matrix = np.zeros((2 * EDGE, EDGE), np.float32)
    for row in range(2 * EDGE):
        centre = row // 2
        beside = min(max(centre - 1 if row % 2 == 0 else centre + 1, 0), EDGE - 1)
        matrix[row, centre] += 0.75
        matrix[row, beside] += 0.25
    return matrix


def plane_weights(parity):
    up = upsample_np()
    out = np.zeros((2, 8, 32, 8, 2, 8, 16), np.float32)
    for core in range(2):
        for yc in range(8):
            row = up[16 * core + 2 * yc + parity]
            for y in range(8):
                out[core, :, :, yc, 0, y, :] = row[8 * core + y] * up[None]
            for x in range(8):
                out[core, x, :, yc, 1, x, :] = row[8 if core == 0 else 7] * up
    return jnp.asarray(out.reshape(2, 8, 256, 256), BF16)


def split_kernel(pos_ref, bricks_ref, send_ref):
    other = 1 - pos_ref[2]
    for x in range(EDGE):
        start = pl.multiple_of(x * 256 + other * 128, 128)
        send_ref[:, x * 128 : x * 128 + 128] = bricks_ref[:, pl.ds(start, 128)]


def split_halves(pos, bricks):
    return pl.pallas_call(
        split_kernel,
        out_shape=jax.ShapeDtypeStruct((128, HALF), BF16),
        in_specs=[pl.BlockSpec(memory_space=pltpu.SMEM), pl.BlockSpec(memory_space=pltpu.VMEM)],
        out_specs=pl.BlockSpec(memory_space=pltpu.VMEM),
        compiler_params=params(),
        name="split_halves",
    )(pos, bricks)


def chip_of(cell):
    return (cell % 64) // 4 * 4 + cell // 4096


def pack_kernel(pos_ref, cell_ref, bricks_ref, other_ref, out_ref, slot_ref, full_ref):
    step = pl.program_id(0)

    @pl.when(step == 0)
    def _():
        core = pos_ref[2]
        dest = chip_of(cell_ref[...])
        across = jnp.broadcast_to(dest, (LOCAL, LOCAL))
        down = across.astype(F32).T.astype(I32)
        earlier = (down == across) & (iota((LOCAL, LOCAL), 0) < iota((LOCAL, LOCAL), 1))
        rank = jnp.sum(earlier.astype(I32), axis=0, keepdims=True) - pos_ref[3] * CAP
        slot_ref[...] = jnp.where((rank >= 0) & (rank < CAP), dest * CAP + rank, -1)
        mine = pl.multiple_of(core * 128, 128)
        theirs = pl.multiple_of(128 - core * 128, 128)
        for x in range(EDGE):
            start = pl.multiple_of(x * 256 + core * 128, 128)
            full_ref[pl.ds(mine, 128), x * 128 : x * 128 + 128] = bricks_ref[:, pl.ds(start, 128)]
        full_ref[pl.ds(theirs, 128), :] = other_ref[...]

    pick = ones_where(iota((128, LOCAL), 0) + step * 128 == slot_ref[...])
    out_ref[...] = nn_dot(pick, full_ref[...]).astype(BF16)


def pack(pos, cell_row, bricks, other):
    rows = CHIPS * CAP
    whole = lambda shape: pl.BlockSpec(shape, lambda s: (0, 0))
    return pl.pallas_call(
        pack_kernel,
        grid=(rows // 128,),
        out_shape=jax.ShapeDtypeStruct((rows, HALF), BF16),
        in_specs=[
            pl.BlockSpec(memory_space=pltpu.SMEM),
            whole((1, LOCAL)),
            whole((128, 2 * HALF)),
            whole((128, HALF)),
        ],
        out_specs=pl.BlockSpec((128, HALF), lambda s: (s, 0)),
        scratch_shapes=[pltpu.VMEM((1, LOCAL), I32), pltpu.VMEM((LOCAL, HALF), BF16)],
        compiler_params=params(semantics=("arbitrary",)),
        name="pack_outbox",
    )(pos, cell_row, bricks, other)


def index_kernel(
    pos_ref, cell_ref, key_z_ref, key_x_ref, place_ref, kz_col_ref, kz_row_ref, kx_col_ref, kx_row_ref, most_ref,
    here_ref, there_ref, slot_ref, dest_ref
):
    plane, z = pos_ref[0], pos_ref[1]
    cell = cell_ref[...]
    gx, gz, gy = cell % 64, cell // 64 % 64, cell // 4096
    dest = chip_of(cell)
    dest_ref[...] = dest
    for_me = dest == plane * 4 + z
    before = ones_where(iota((LOCAL, LOCAL), 0) < iota((LOCAL, LOCAL), 1))
    rank = nn_dot(ones_where(for_me), before).astype(I32) - pos_ref[3] * CAP
    group = iota((CHIPS, LOCAL), 0) % 8
    slot_ref[...] = jnp.where(for_me & (rank >= 0) & (rank < CAP), rank + group * CAP, -1)
    here_ref[...] = jnp.where(for_me, gz * 4 + gx % 4, -1)
    there_ref[...] = jnp.where((gy == z) & (gz // 4 == plane), gx // 4 * 16 + gz % 4 * 4 + gx % 4, -1)
    down = iota((LOCAL, LOCAL), 0)
    down_slot = iota((128, LOCAL), 0)
    down_chip = iota((CHIPS, LOCAL), 0)
    units = jnp.ones((LOCAL, 128), BF16)
    byte = iota((8, LOCAL), 0)

    def key_bytes(row):
        return jnp.where(
            byte == 0, row % 256, jnp.where(byte == 1, row // 256 % 256, jnp.where(byte == 2, row // 65536, 0))
        ).astype(F32).astype(BF16)

    key_z_sum = jnp.zeros((LOCAL, 8), F32)
    key_x_sum = jnp.zeros((LOCAL, 8), F32)
    most = jnp.zeros((CHIPS, 128), F32)
    for part in range(8):

        def source(index, carry):
            place, key_z_sum, key_x_sum, most = carry
            row = pl.ds(part * 8 + index, 1)
            here = ones_where(down == here_ref[row, :])
            there = ones_where(down == there_ref[row, :])
            place = place + nt_dot(here, ones_where(down_slot == slot_ref[row, :]))
            key_z_sum = key_z_sum + nt_dot(here, key_bytes(key_z_ref[row, :]))
            key_x_sum = key_x_sum + nt_dot(there, key_bytes(key_x_ref[row, :]))
            most = jnp.maximum(most, nn_dot(ones_where(down_chip == dest_ref[row, :]), units))
            return place, key_z_sum, key_x_sum, most

        place, key_z_sum, key_x_sum, most = lax.fori_loop(
            0, 8, source, (jnp.zeros((LOCAL, 128), F32), key_z_sum, key_x_sum, most)
        )
        place_ref[:, part * 128 : part * 128 + 128] = place.astype(BF16)
    most_ref[...] = most
    for sums, col_ref, row_ref in ((key_z_sum, kz_col_ref, kz_row_ref), (key_x_sum, kx_col_ref, kx_row_ref)):
        col = sums[:, 0:1] + 256.0 * sums[:, 1:2] + 65536.0 * sums[:, 2:3]
        wide = jnp.broadcast_to(col, (LOCAL, 128))
        col_ref[...] = wide
        row_ref[...] = wide.T[0:8]


def index_maps(pos, cell, key_z, key_x):
    vmem = pl.BlockSpec(memory_space=pltpu.VMEM)
    col = jax.ShapeDtypeStruct((LOCAL, 128), F32)
    row = jax.ShapeDtypeStruct((8, LOCAL), F32)
    return pl.pallas_call(
        index_kernel,
        out_shape=(
            jax.ShapeDtypeStruct((LOCAL, CHIPS * CAP), BF16),
            col,
            row,
            col,
            row,
            jax.ShapeDtypeStruct((CHIPS, 128), F32),
        ),
        in_specs=[pl.BlockSpec(memory_space=pltpu.SMEM), vmem, vmem, vmem],
        out_specs=(vmem,) * 6,
        scratch_shapes=[pltpu.VMEM((CHIPS, LOCAL), I32)] * 4,
        compiler_params=params(),
        cost_estimate=pl.CostEstimate(flops=10**10, bytes_accessed=10**6, transcendentals=0),
        name="index_maps",
    )(pos, cell, key_z, key_x)


def unpack_kernel(pos_ref, place_ref, recv_ref, cells_ref, edge_ref):
    step = pl.program_id(0)
    cells = nn_dot(place_ref[...], recv_ref[...]).astype(BF16)
    cells_ref[...] = cells
    width = cells.shape[1]
    row = iota((width, 256), 0)
    lane = iota((width, 256), 1)
    first = jnp.where(pos_ref[2] == 0, 112, 0)
    x = row // 128 + step * (width // 128)
    pick = ones_where((row % 128 - first == lane % 16) & (x == lane // 16))
    edge = nn_dot(cells, pick).astype(BF16)

    @pl.when(step == 0)
    def _():
        edge_ref[...] = edge

    @pl.when(step > 0)
    def _():
        edge_ref[...] += edge


def unpack(pos, place, received):
    rows = CHIPS * CAP
    width = 512
    return pl.pallas_call(
        unpack_kernel,
        grid=(HALF // width,),
        out_shape=(jax.ShapeDtypeStruct((LOCAL, HALF), BF16), jax.ShapeDtypeStruct((LOCAL, 256), BF16)),
        in_specs=[
            pl.BlockSpec(memory_space=pltpu.SMEM),
            pl.BlockSpec((LOCAL, rows), lambda s: (0, 0)),
            pl.BlockSpec((rows, width), lambda s: (0, s)),
        ],
        out_specs=(pl.BlockSpec((LOCAL, width), lambda s: (0, s)), pl.BlockSpec((LOCAL, 256), lambda s: (0, 0))),
        compiler_params=params(semantics=("arbitrary",)),
        name="unpack_inbox",
    )(pos, place, received)


def render_kernel(pos_ref, transfer_ref, cells_ref, edge_ref, weights_ref, tile_x_ref, tile_z_ref, plane_ref, state_ref):
    for x in range(EDGE):
        side = x // 8 * 128
        operand = jnp.concatenate([cells_ref[:, x * 128 : x * 128 + 128], edge_ref[:, side : side + 128]], axis=1)
        plane_ref[x] = nt_dot(weights_ref[0, x % 8], operand).reshape(32, 8, 128)
    slope = [transfer_ref[0, 0] * LOG2E] + [0.5 * transfer_ref[0, c] for c in (1, 2, 3)]
    offset = [transfer_ref[1, 0] * LOG2E] + [0.5 * transfer_ref[1, c] for c in (1, 2, 3)]
    zero = jnp.zeros((8, 128), F32)
    one = jnp.ones((8, 128), F32)
    state_ref[0] = jnp.ones((32, 8, 128), F32)
    for n in range(1, 5):
        state_ref[n] = jnp.zeros((32, 8, 128), F32)

    def classify(sample):
        grown = jnp.exp2(slope[0] * sample + offset[0])
        above = 1.0 + grown
        lost = jnp.minimum(grown, 1.0) - (jnp.minimum(above, 2.0) - 1.0)
        dense = jnp.log2(above) + LOG2E * lost
        alpha = dense * (KAPPA - dense * (KAPPA * KAPPA / 2 - dense * (KAPPA * KAPPA * KAPPA / 6)))
        return dense, alpha, [jnp.tanh(slope[c] * sample + offset[c]) for c in (1, 2, 3)]

    def advance(state, values):
        dense, alpha, colours = values
        weight = alpha * state[0]
        return (
            state[0] - weight,
            state[1] + colours[0] * weight,
            state[2] + colours[1] * weight,
            state[3] + colours[2] * weight,
            state[4] + dense,
        )

    def result(state):
        depth = KAPPA * state[4]
        half = jnp.tanh(0.5 * depth)
        total = half / (1.0 + half)
        return [total + 0.5 * state[1], total + 0.5 * state[2], total + 0.5 * state[3], depth]

    unroll = 8

    def slab(x, carry):
        left = jnp.maximum(x - 1, 0)
        right = jnp.minimum(x + 1, EDGE - 1)

        def columns(block, views):
            view_even, view_odd = views
            for step in range(unroll):
                k = block * unroll + step
                centre = 0.75 * plane_ref[x, k]
                even = classify(centre + 0.25 * plane_ref[left, k])
                odd = classify(centre + 0.25 * plane_ref[right, k])
                view_even = advance(view_even, even)
                view_odd = advance(view_odd, odd)
                state = tuple(state_ref[n, k] for n in range(5))
                state = advance(advance(state, even), odd)
                for n in range(5):
                    state_ref[n, k] = state[n]
            return view_even, view_odd

        start = (one, zero, zero, zero, zero)
        views = lax.fori_loop(0, 32 // unroll, columns, (start, start))
        for odd in range(2):
            values = result(views[odd])
            for c in range(4):
                tile_z_ref[c, 2 * x + odd] = values[c]
        return carry

    lax.fori_loop(0, EDGE, slab, 0)
    values = result([state_ref[n] for n in range(5)])
    for c in range(4):
        tile_x_ref[:, c * 256 : c * 256 + 256] = values[c].reshape(256, 128).T


def render(pos, transfer, cells, edge, weights):
    smem = pl.BlockSpec(memory_space=pltpu.SMEM)
    grid_spec = pltpu.PrefetchScalarGridSpec(
        num_scalar_prefetch=1,
        grid=(2,),
        in_specs=[
            smem,
            pl.BlockSpec((128, HALF), lambda g, pos: (g, 0)),
            pl.BlockSpec((128, 256), lambda g, pos: (g, 0)),
            pl.BlockSpec((1, 8, 256, 256), lambda g, pos: (pos[2], 0, 0, 0)),
        ],
        out_specs=(
            pl.BlockSpec((128, 1024), lambda g, pos: (g, 0)),
            pl.BlockSpec((4, 32, 8, 128), lambda g, pos: (0, 0, 0, g)),
        ),
        scratch_shapes=[pltpu.VMEM((EDGE, 32, 8, 128), F32), pltpu.VMEM((5, 32, 8, 128), F32)],
    )
    return pl.pallas_call(
        render_kernel,
        grid_spec=grid_spec,
        out_shape=(jax.ShapeDtypeStruct((LOCAL, 1024), F32), jax.ShapeDtypeStruct((4, 32, 8, LOCAL), F32)),
        compiler_params=params(semantics=("arbitrary",)),
        cost_estimate=pl.CostEstimate(flops=10**10, bytes_accessed=10**7, transcendentals=10**7),
        name="render_bricks",
    )(pos, transfer, cells, edge, weights)


def compose_z_kernel(col_ref, row_ref, first_ref, second_ref, out_ref):
    here = iota((LOCAL, LOCAL), 0)
    there = iota((LOCAL, LOCAL), 1)
    col = jnp.concatenate([col_ref[...], col_ref[...]], axis=1)
    ahead = ones_where((col < row_ref[0:1, :]) & (here % 4 == there % 4))
    group = ones_where(iota((8, LOCAL), 0) == iota((8, LOCAL), 1) % 4)
    for parity, tile_ref in enumerate((first_ref, second_ref)):
        depth = tile_ref[3].reshape(256, LOCAL)
        pieces = parts_of(depth, 3)
        through = jnp.exp(-sum(nn_dot(piece, ahead) for piece in pieces))
        for c in range(4):
            values = depth if c == 3 else tile_ref[c].reshape(256, LOCAL) * through
            out_ref[:, parity * 1024 + c * 256 : parity * 1024 + c * 256 + 256] = sum(
                nt_dot(group, piece) for piece in (pieces if c == 3 else parts_of(values, 3))
            )


def compose_z(col, row, first, second):
    return pl.pallas_call(
        compose_z_kernel,
        out_shape=jax.ShapeDtypeStruct((8, 2048), F32),
        in_specs=[pl.BlockSpec(memory_space=pltpu.VMEM)] * 4,
        out_specs=pl.BlockSpec(memory_space=pltpu.VMEM),
        compiler_params=params(),
        cost_estimate=pl.CostEstimate(flops=10**9, bytes_accessed=4 * 10**6, transcendentals=10**5),
        name="compose_z",
    )(col, row, first, second)


def compose_x_kernel(col_ref, row_ref, tile_ref, out_ref):
    here = iota((LOCAL, LOCAL), 0)
    there = iota((LOCAL, LOCAL), 1)
    col = jnp.concatenate([col_ref[...], col_ref[...]], axis=1)
    ahead = ones_where((row_ref[0:1, :] < col) & (here // 4 % 4 == there // 4 % 4))
    group = ones_where(iota((8, LOCAL), 0) == iota((8, LOCAL), 1) // 4 % 4)
    depth = tile_ref[:, 768:1024]
    pieces = parts_of(depth, 3)
    through = jnp.exp(-sum(nn_dot(ahead, piece) for piece in pieces))
    for c in range(4):
        values = depth if c == 3 else tile_ref[:, c * 256 : c * 256 + 256] * through
        out_ref[:, c * 256 : c * 256 + 256] = sum(
            nn_dot(group, piece) for piece in (pieces if c == 3 else parts_of(values, 3))
        )


def compose_x(col, row, tiles):
    return pl.pallas_call(
        compose_x_kernel,
        out_shape=jax.ShapeDtypeStruct((8, 1024), F32),
        in_specs=[pl.BlockSpec(memory_space=pltpu.VMEM)] * 3,
        out_specs=pl.BlockSpec(memory_space=pltpu.VMEM),
        compiler_params=params(),
        cost_estimate=pl.CostEstimate(flops=10**9, bytes_accessed=10**6, transcendentals=10**5),
        name="compose_x",
    )(col, row, tiles)


def to_frame(sums):
    picture = sums[:4].reshape(4, 2, 4, 32, 8).transpose(2, 4, 1, 0, 3).reshape(4, 16, 128)
    return jnp.concatenate([picture[:3], -jnp.expm1(-picture[3:])], axis=0)


def swap_cores(values):
    return lax.ppermute(values, "c", [(0, 1), (1, 0)])


def body(bricks, transfer, assignment, brick_cell, depth_rank):
    plane = lax.axis_index(PLANE)
    z = lax.axis_index("z")
    core = lax.axis_index("c")
    chip = plane * 4 + z

    def position(turn):
        return jnp.stack([plane, z, core, turn]).astype(I32)

    start = position(jnp.int32(0))
    cell = brick_cell.reshape(CHIPS, LOCAL)
    cell_row = lax.dynamic_slice_in_dim(cell, chip, 1)
    major = assignment.reshape(CHIPS, LOCAL) * 16384
    key_z = major + depth_rank[0].reshape(CHIPS, LOCAL)
    key_x = major + depth_rank[1].reshape(CHIPS, LOCAL)

    other = swap_cores(split_halves(start, bricks))

    def deliver(pos, place):
        outbox = pack(pos, cell_row, bricks, other).reshape(CHIPS, CAP, HALF)
        received = lax.all_to_all(outbox, CHIP, split_axis=0, concat_axis=0, tiled=True)
        return unpack(pos, place, received.reshape(CHIPS * CAP, HALF))

    place, kz_col, kz_row, kx_col, kx_row, most = index_maps(start, cell, key_z, key_x)
    cells, edge = deliver(start, place)
    rounds = (jnp.max(most).astype(I32) + CAP - 1) // CAP

    def next_round(carry):
        turn, cells, edge = carry
        pos = position(turn)
        more_cells, more_edge = deliver(pos, index_maps(pos, cell, key_z, key_x)[0])
        return turn + 1, cells + more_cells, edge + more_edge

    _, cells, edge = lax.while_loop(lambda carry: carry[0] < rounds, next_round, (jnp.int32(1), cells, edge))

    edge = swap_cores(edge)
    tiles_z = []
    sums_x = []
    for parity in range(2):
        tile_x, tile_z = render(start, transfer, cells, edge, plane_weights(parity))
        tiles_z.append(tile_z)
        landed = lax.all_to_all(tile_x.reshape(16, 16, 1024), PLANE, split_axis=0, concat_axis=0, tiled=True)
        sums_x.append(compose_x(kx_col, kx_row, landed.reshape(LOCAL, 1024)))
    sums_z = compose_z(kz_col, kz_row, tiles_z[0], tiles_z[1])
    return to_frame(sums_z), to_frame(jnp.concatenate(sums_x, axis=1))


def solution(mesh):
    fine = Mesh(mesh.devices.reshape(4, 4, 4, 2), ("y", "x", "z", "c"))
    in_specs = (P(("y", "x", "z", "c"), None), P(), P(), P(), P())
    out_specs = (P(None, ("z", "c"), PLANE), P(None, ("z", "c"), PLANE))
    return jax.shard_map(body, mesh=fine, in_specs=in_specs, out_specs=out_specs, check_vma=False)
```

```python
import functools

import jax
import jax.numpy as jnp
import numpy as np
from jax import lax
from jax.experimental import pallas as pl
from jax.experimental.pallas import tpu as pltpu
from jax.sharding import Mesh
from jax.sharding import PartitionSpec as P

SIDE = 1024
EDGE = 16
CAP = 8
TRIES = 5
GROUP = 8
CLASSES = 4
BACK = 8
CHIPS = 64
LOCAL = 256
HALF = EDGE * EDGE * EDGE // 2
F32 = jnp.float32
BF16 = jnp.bfloat16
I32 = jnp.int32
LOG2E = 1.4426950408889634
KAPPA = 2.0 * 0.6931471805599453 / SIDE
PLANE = ("y", "x1", "x0")
CHIP = ("y", "x1", "x0", "z")
NEAR = ("x0", "z")


TOP = 32767.0
LOG_MID = -9.88
LOG_REACH = 9.3


def iota(shape, axis):
    return lax.broadcasted_iota(I32, shape, axis)


def ones_where(mask):
    return jnp.where(mask, 1.0, 0.0).astype(BF16)


def nt_dot(left, right):
    return lax.dot_general(left, right, (((1,), (1,)), ((), ())), preferred_element_type=F32)


def nn_dot(left, right):
    return jnp.dot(left, right, preferred_element_type=F32)


def opacity(depth):
    half = jnp.tanh(0.5 * depth)
    return 2.0 * half / (1.0 + half)


def parts_of(values, count):
    pieces = []
    rest = values
    for _ in range(count - 1):
        piece = rest.astype(BF16)
        pieces.append(piece)
        rest = rest - piece.astype(F32)
    return pieces + [rest.astype(BF16)]


def in_hbm(array):
    return pltpu.with_memory_space_constraint(array, pltpu.HBM)


def params(mib=24, semantics=None):
    return pltpu.CompilerParams(vmem_limit_bytes=mib * 1024 * 1024, dimension_semantics=semantics)


def upsample_np():
    matrix = np.zeros((2 * EDGE, EDGE), np.float32)
    for row in range(2 * EDGE):
        centre = row // 2
        beside = min(max(centre - 1 if row % 2 == 0 else centre + 1, 0), EDGE - 1)
        matrix[row, centre] += 0.75
        matrix[row, beside] += 0.25
    return matrix


def plane_weights(batch):
    up = upsample_np()
    out = np.zeros((2, 32, 8, 1 + batch, 8, 16), np.float32)
    for core in range(2):
        for sub in range(8):
            centre = 4 * batch + sub // 2
            beside = max(centre - 1, 0) if sub % 2 == 0 else centre + 1
            for m, share in ((centre, 0.75), (beside, 0.25)):
                half, y = m // 8, m % 8
                out[core, :, sub, half, y if core == 0 else 7 - y] += 0.25 * share * up
    return jnp.asarray(out.reshape(2, 256, 128 * (1 + batch)), BF16)


def split_kernel(pos_ref, bricks_ref, send_ref):
    other = 1 - pos_ref[2]
    for x in range(EDGE):
        start = pl.multiple_of(x * 256 + other * 128, 128)
        send_ref[:, x * 128 : x * 128 + 128] = bricks_ref[:, pl.ds(start, 128)]


def split_halves(pos, bricks):
    return pl.pallas_call(
        split_kernel,
        out_shape=jax.ShapeDtypeStruct((128, HALF), BF16),
        in_specs=[pl.BlockSpec(memory_space=pltpu.SMEM), pl.BlockSpec(memory_space=pltpu.VMEM)],
        out_specs=pl.BlockSpec(memory_space=pltpu.VMEM),
        compiler_params=params(),
        name="split_halves",
    )(pos, bricks)


def chip_of(cell):
    return (cell % 64) // 4 * 4 + cell // 4096


def up(values, shift):
    inside = iota(values.shape, 1) % GROUP + shift < GROUP
    return jnp.where(inside, pltpu.roll(values, 128 - shift, axis=1), pltpu.roll(values, GROUP - shift, axis=1))


def shift_of(turn, kind):
    return 1 + (turn + 2 * kind) % (GROUP - 1)


def by_class(values, kinds, turn, back):
    out = None
    for kind in range(CLASSES):
        shift = shift_of(turn, kind)
        moved = up(values, GROUP - shift if back else shift)
        out = moved if out is None else jnp.where(kinds == kind, moved, out)
    return out


def relay_plan(counts, kinds):
    over = jnp.maximum(counts - CAP, 0.0)
    taken = jnp.minimum(counts, CAP)
    begin = jnp.zeros_like(over)
    amounts, starts, bases = [], [begin], []
    for turn in range(TRIES):
        amount = jnp.minimum(over, CAP - by_class(taken, kinds, turn, False))
        bases.append(taken)
        taken = taken + by_class(amount, kinds, turn, True)
        over = over - amount
        begin = begin + amount
        amounts.append(amount)
        starts.append(begin)
    return amounts, starts, bases, over


def pack_kernel(
    pos_ref, cell_ref, bricks_ref, other_ref, out_ref, full_ref, box_ref, sems
):
    core = pos_ref[2]
    turn = pos_ref[3]
    kind = (pos_ref[0] * 4 + pos_ref[1]) % CLASSES
    dest = chip_of(cell_ref[...])
    across = jnp.broadcast_to(dest, (LOCAL, LOCAL))
    down = across.astype(F32).T.astype(I32)
    earlier = (down == across) & (iota((LOCAL, LOCAL), 0) < iota((LOCAL, LOCAL), 1))
    rank = jnp.sum(earlier.astype(I32), axis=0, keepdims=True)
    later = rank - turn * CAP
    in_turn = jnp.where((later >= 0) & (later < CAP), dest * CAP + later, -1)
    chips = iota((128, LOCAL), 0)
    counts = nt_dot(jnp.ones((8, LOCAL), BF16), ones_where(chips % CHIPS == dest))
    kinds = jnp.full((8, 128), kind, I32)
    _, starts, bases, _ = relay_plan(counts, kinds)
    rows = starts[1:] + [by_class(base, kinds, n, False) for n, base in enumerate(bases)]
    table = jnp.concatenate([row[0:1] for row in rows] + [jnp.zeros((16 - len(rows), 128), F32)], axis=0)
    found = nn_dot(table.astype(BF16), ones_where(chips == dest)).astype(I32)
    relayed = jnp.where(rank < CAP, dest * CAP + rank, -1)
    over = rank - CAP
    for n in range(TRIES):
        begin = found[n - 1 : n] if n else jnp.zeros_like(over)
        inside = (over >= begin) & (over < found[n : n + 1])
        relay = dest // GROUP * GROUP + (dest + shift_of(n, kind)) % GROUP
        relayed = jnp.where(inside, relay * CAP + found[TRIES + n : TRIES + n + 1] + over - begin, relayed)
    slot = jnp.where(turn < 0, relayed, in_turn)
    mine = pl.multiple_of(core * 128, 128)
    theirs = pl.multiple_of(128 - core * 128, 128)
    for x in range(EDGE):
        start = pl.multiple_of(x * 256 + core * 128, 128)
        full_ref[pl.ds(mine, 128), x * 128 : x * 128 + 128] = bricks_ref[:, pl.ds(start, 128)]
    full_ref[pl.ds(theirs, 128), :] = other_ref[...]
    copies = []
    for block in range(CHIPS * CAP // 128):
        pick = ones_where(iota((128, LOCAL), 0) + block * 128 == slot)
        rows = pl.ds(block * 128, 128)
        box_ref[rows, :] = nn_dot(pick, full_ref[...]).astype(BF16)
        copy = pltpu.make_async_copy(box_ref.at[rows, :], out_ref.at[rows, :], sems.at[block])
        copy.start()
        copies.append(copy)
    for copy in copies:
        copy.wait()


def pack(pos, cell_row, bricks, other):
    rows = CHIPS * CAP
    grid_spec = pltpu.PrefetchScalarGridSpec(
        num_scalar_prefetch=1,
        grid=(1,),
        in_specs=[
            pl.BlockSpec((1, LOCAL), lambda s, pos: (0, 0)),
            pl.BlockSpec((128, 2 * HALF), lambda s, pos: (0, 0)),
            pl.BlockSpec((128, HALF), lambda s, pos: (0, 0)),
        ],
        out_specs=pl.BlockSpec(memory_space=pltpu.HBM),
        scratch_shapes=[
            pltpu.VMEM((LOCAL, HALF), BF16),
            pltpu.VMEM((rows, HALF), BF16),
            pltpu.SemaphoreType.DMA((rows // 128,)),
        ],
    )
    return pl.pallas_call(
        pack_kernel,
        grid_spec=grid_spec,
        out_shape=pltpu.HBM((rows, HALF), BF16),
        compiler_params=params(),
        name="pack_outbox",
    )(pos, cell_row, bricks, other)


def index_kernel(
    pos_ref, cell_ref, place_ref, relay_place_ref, forward_ref, most_ref,
    here_ref, slot_ref, relay_ref, dest_ref, count_ref, side_ref
):
    plane, z, turn = pos_ref[0], pos_ref[1], pos_ref[3]
    me = plane * 4 + z
    mine = me % GROUP
    first = me - mine
    cell = cell_ref[...]
    gx, gz = cell % 64, cell // 64 % 64
    dest = chip_of(cell)
    dest_ref[...] = dest
    down_128 = iota((128, LOCAL), 0)
    down_chip = down_128 % CHIPS
    units = jnp.ones((8, LOCAL), BF16)

    def count(index, carry):
        row = pl.ds(index, 1)
        count_ref[row, :] = nt_dot(units, ones_where(down_chip == dest_ref[row, :]))[0:1]
        return carry

    lax.fori_loop(0, CHIPS, count, 0, unroll=8)
    counts = count_ref[...]
    most_ref[0] = jnp.max(counts).astype(I32)
    kinds = iota((CHIPS, 128), 0) % CLASSES
    amounts, starts, bases, left = relay_plan(counts, kinds)
    sources = ones_where(iota((CHIPS, CHIPS), 1) < iota((CHIPS, CHIPS), 0))
    lane = iota((CHIPS, 128), 1)

    def column(values, chip):
        return jnp.sum(jnp.where(lane == chip, values, 0.0), axis=1, keepdims=True)

    for_me = dest == me
    before = ones_where(iota((LOCAL, LOCAL), 0) < iota((LOCAL, LOCAL), 1))
    rank = nn_dot(ones_where(for_me), before).astype(I32)
    over = rank - CAP
    slots = CHIPS * CAP
    spread = jnp.where(iota((CHIPS, slots), 1) // CAP == iota((CHIPS, slots), 0), 1.0, 0.0)
    along = lambda col: jnp.sum(col * spread, axis=0, keepdims=True).astype(I32)
    slot_lane = iota((1, slots), 1) % CAP
    relay = jnp.full((CHIPS, LOCAL), -1, I32)
    handed = jnp.full((1, slots), -1, I32)
    for shift in range(1, GROUP):
        amount = jnp.zeros((CHIPS, 128), F32)
        begin = amount
        base = amount
        for kind in range(CLASSES):
            for n in range(TRIES):
                if shift_of(n, kind) == shift:
                    amount = jnp.where(kinds == kind, amounts[n], amount)
                    begin = jnp.where(kinds == kind, starts[n], begin)
                    base = jnp.where(kinds == kind, bases[n], base)
        prefix = nn_dot(sources, amount.astype(BF16))
        left = left + jnp.maximum(jnp.sum(amount, axis=0, keepdims=True) - BACK, 0.0)
        order = over - column(begin, me).astype(I32)
        at = (mine + shift) % GROUP * BACK + column(prefix, me).astype(I32) + order
        relay = jnp.where((order >= 0) & (order < column(amount, me).astype(I32)), at, relay)
        near = (mine + GROUP - shift) % GROUP
        order = slot_lane - along(column(base, me))
        at = near * BACK + order + along(column(prefix, first + near))
        handed = jnp.where((order >= 0) & (order < along(column(amount, first + near))), at, handed)
    forward_ref[...] = ones_where(iota((GROUP * BACK, slots), 0) == handed)
    most_ref[1] = jnp.max(left).astype(I32)
    relay_ref[...] = jnp.where(for_me & (turn < 0), relay, -1)
    group = iota((CHIPS, LOCAL), 0) % (128 // CAP)
    later = rank - jnp.maximum(turn, 0) * CAP
    slot_ref[...] = jnp.where(for_me & (later >= 0) & (later < CAP), later + group * CAP, -1)
    here_ref[...] = jnp.where(for_me, gz * 4 + gx % 4, -1)
    down_256 = iota((LOCAL, LOCAL), 0)
    side_ref[...] = jnp.zeros((LOCAL, 128), F32)
    for part in range(slots // 128):

        def source(index, place):
            row = pl.ds(part * (128 // CAP) + index, 1)
            here = ones_where(down_256 == here_ref[row, :])
            wanted = jnp.concatenate(
                [ones_where(down_128 == slot_ref[row, :]), ones_where(down_128 == relay_ref[row, :])], axis=0
            )
            both = nt_dot(here, wanted)
            side_ref[...] += both[:, 128:]
            return place + both[:, :128]

        place = lax.fori_loop(0, 128 // CAP, source, jnp.zeros((LOCAL, 128), F32), unroll=4)
        place_ref[:, part * 128 : part * 128 + 128] = place.astype(BF16)
    relay_place_ref[...] = side_ref[...].astype(BF16)


def index_maps(pos, cell):
    vmem = pl.BlockSpec(memory_space=pltpu.VMEM)
    return pl.pallas_call(
        index_kernel,
        out_shape=(
            pltpu.HBM((LOCAL, CHIPS * CAP), BF16),
            pltpu.HBM((LOCAL, 128), BF16),
            jax.ShapeDtypeStruct((GROUP * BACK, CHIPS * CAP), BF16),
            jax.ShapeDtypeStruct((2,), I32),
        ),
        in_specs=[pl.BlockSpec(memory_space=pltpu.SMEM), vmem],
        grid=(1,),
        out_specs=(
            pl.BlockSpec((LOCAL, CHIPS * CAP), lambda s: (0, 0)),
            pl.BlockSpec((LOCAL, 128), lambda s: (0, 0)),
            pl.BlockSpec((GROUP * BACK, CHIPS * CAP), lambda s: (0, 0)),
            pl.BlockSpec(memory_space=pltpu.SMEM),
        ),
        scratch_shapes=[pltpu.VMEM((CHIPS, LOCAL), I32)] * 4
        + [pltpu.VMEM((CHIPS, 128), F32), pltpu.VMEM((LOCAL, 128), F32)],
        compiler_params=params(),
        cost_estimate=pl.CostEstimate(flops=10**10, bytes_accessed=10**6, transcendentals=0),
        name="index_maps",
    )(pos, cell)


def key_kernel(pos_ref, cell_ref, key_z_ref, key_x_ref, kz_col_ref, kz_row_ref, kx_col_ref, kx_row_ref, here_ref, there_ref):
    plane, z = pos_ref[0], pos_ref[1]
    cell = cell_ref[...]
    gx, gz, gy = cell % 64, cell // 64 % 64, cell // 4096
    here_ref[...] = jnp.where((gy == z) & (gx // 4 == plane), gz * 4 + gx % 4, -1)
    there_ref[...] = jnp.where((gy == z) & (gz // 4 == plane), gx // 4 * 16 + gz % 4 * 4 + gx % 4, -1)
    down = iota((LOCAL, LOCAL), 0)
    byte = iota((8, LOCAL), 0)

    def key_bytes(row):
        return jnp.where(
            byte == 0, row % 256, jnp.where(byte == 1, row // 256 % 256, jnp.where(byte == 2, row // 65536, 0))
        ).astype(F32).astype(BF16)

    def source(index, sums):
        row = pl.ds(index, 1)
        return (
            sums[0] + nt_dot(ones_where(down == here_ref[row, :]), key_bytes(key_z_ref[row, :])),
            sums[1] + nt_dot(ones_where(down == there_ref[row, :]), key_bytes(key_x_ref[row, :])),
        )

    nothing = jnp.zeros((LOCAL, 8), F32)
    sums = lax.fori_loop(0, CHIPS, source, (nothing, nothing), unroll=4)
    for part, col_ref, row_ref in ((sums[0], kz_col_ref, kz_row_ref), (sums[1], kx_col_ref, kx_row_ref)):
        col = part[:, 0:1] + 256.0 * part[:, 1:2] + 65536.0 * part[:, 2:3]
        wide = jnp.broadcast_to(col, (LOCAL, 128))
        col_ref[...] = wide
        row_ref[...] = wide.T[0:8]


def order_keys(pos, cell, key_z, key_x):
    vmem = pl.BlockSpec(memory_space=pltpu.VMEM)
    col = jax.ShapeDtypeStruct((LOCAL, 128), F32)
    row = jax.ShapeDtypeStruct((8, LOCAL), F32)
    return pl.pallas_call(
        key_kernel,
        out_shape=(col, row, col, row),
        in_specs=[pl.BlockSpec(memory_space=pltpu.SMEM), vmem, vmem, vmem],
        out_specs=(vmem,) * 4,
        scratch_shapes=[pltpu.VMEM((CHIPS, LOCAL), I32)] * 2,
        compiler_params=params(),
        cost_estimate=pl.CostEstimate(flops=10**10, bytes_accessed=10**6, transcendentals=0),
        name="order_keys",
    )(pos, cell, key_z, key_x)


def forward_kernel(forward_ref, recv_ref, out_ref):
    out_ref[...] = nn_dot(forward_ref[...], recv_ref[...]).astype(BF16)


def forward(maps, received):
    vmem = pl.BlockSpec(memory_space=pltpu.VMEM)
    handed = pl.pallas_call(
        forward_kernel,
        out_shape=jax.ShapeDtypeStruct((GROUP * BACK, HALF), BF16),
        in_specs=[vmem, vmem],
        out_specs=vmem,
        compiler_params=params(),
        cost_estimate=pl.CostEstimate(flops=10**8, bytes_accessed=10**6, transcendentals=0),
        name="hand_on",
    )(maps, received)
    sent = lax.all_to_all(handed.reshape(GROUP, BACK, HALF), NEAR, split_axis=0, concat_axis=0, tiled=True)
    return sent.reshape(GROUP * BACK, HALF)


def unpack_kernel(place_ref, relay_ref, recv_ref, back_ref, cells_ref):
    cells = nn_dot(place_ref[...], recv_ref[...]) + nn_dot(relay_ref[:, : GROUP * BACK], back_ref[...])
    cells_ref[...] = cells.astype(BF16)


def unpack(place, relay_place, received, back):
    rows, lanes = received.shape
    width = 512
    return pl.pallas_call(
        unpack_kernel,
        grid=(lanes // width,),
        out_shape=pltpu.HBM((LOCAL, lanes), BF16),
        in_specs=[
            pl.BlockSpec((LOCAL, rows), lambda s: (0, 0)),
            pl.BlockSpec((LOCAL, 128), lambda s: (0, 0)),
            pl.BlockSpec((rows, width), lambda s: (0, s)),
            pl.BlockSpec((GROUP * BACK, width), lambda s: (0, s)),
        ],
        out_specs=pl.BlockSpec((LOCAL, width), lambda s: (0, s)),
        compiler_params=params(semantics=("arbitrary",)),
        cost_estimate=pl.CostEstimate(flops=10**9, bytes_accessed=3 * 10**6, transcendentals=0),
        name="unpack_inbox",
    )(in_hbm(place), in_hbm(relay_place), received, back)


def render_kernel(batch, pos_ref, transfer_ref, *refs):
    halves, (weights_ref, tile_x_ref, tile_z_ref, plane_ref, state_ref) = refs[: 1 + batch], refs[1 + batch :]
    weights = weights_ref[pos_ref[2]]
    for x in range(EDGE):
        operand = jnp.concatenate([ref[:, x * 128 : x * 128 + 128] for ref in halves], axis=1)
        plane_ref[x] = nt_dot(weights, operand).reshape(32, 8, 128)
    slope = [transfer_ref[0, 0] * LOG2E] + [0.5 * transfer_ref[0, c] for c in (1, 2, 3)]
    offset = [transfer_ref[1, 0] * LOG2E] + [0.5 * transfer_ref[1, c] for c in (1, 2, 3)]
    zero = jnp.zeros((8, 128), F32)
    one = jnp.ones((8, 128), F32)
    state_ref[0] = jnp.ones((32, 8, 128), F32)
    for n in range(1, 5):
        state_ref[n] = jnp.zeros((32, 8, 128), F32)

    def classify(sample):
        grown = jnp.exp2(slope[0] * sample + offset[0])
        above = 1.0 + grown
        dense = jnp.log2(above) * (grown * pl.reciprocal(above - 1.0, approx=True))
        alpha = dense * (KAPPA - dense * (KAPPA * KAPPA / 2 - dense * (KAPPA * KAPPA * KAPPA / 6)))
        return dense, alpha, [jnp.tanh(slope[c] * sample + offset[c]) for c in (1, 2, 3)]

    def advance(state, values):
        dense, alpha, colours = values
        weight = alpha * state[0]
        return (
            state[0] - weight,
            state[1] + colours[0] * weight,
            state[2] + colours[1] * weight,
            state[3] + colours[2] * weight,
            state[4] + dense,
        )

    def result(state):
        depth = KAPPA * state[4]
        half = 0.5 * opacity(depth)
        return [half + 0.5 * state[1], half + 0.5 * state[2], half + 0.5 * state[3], depth]

    def coded(state):
        depth = KAPPA * state[4]
        scale = TOP / opacity(depth)
        codes = [jnp.floor(scale * state[c] + 0.5) for c in (1, 2, 3)]
        codes.append(jnp.floor((jnp.log2(depth) - LOG_MID) * (TOP / LOG_REACH) + 0.5))
        return [jnp.clip(code, -TOP, TOP) for code in codes]

    def slab(x, carry):
        left = jnp.maximum(x - 1, 0)
        right = jnp.minimum(x + 1, EDGE - 1)

        def columns(view_even, view_odd):
            for k in range(32):
                centre = 3.0 * plane_ref[x, k]
                even = classify(centre + plane_ref[left, k])
                odd = classify(centre + plane_ref[right, k])
                view_even = advance(view_even, even)
                view_odd = advance(view_odd, odd)
                state = tuple(state_ref[n, k] for n in range(5))
                state = advance(advance(state, even), odd)
                for n in range(5):
                    state_ref[n, k] = state[n]
            return view_even, view_odd

        start = (one, zero, zero, zero, zero)
        views = columns(start, start)
        for odd in range(2):
            values = result(views[odd])
            for c in range(4):
                tile_z_ref[c, 2 * x + odd] = values[c]
        return carry

    lax.fori_loop(0, EDGE, slab, 0)
    values = coded([state_ref[n] for n in range(5)])
    for c in range(4):
        tile_x_ref[:, c * 256 : c * 256 + 256] = values[c].reshape(256, 128).T.astype(I32).astype(jnp.int16)


def render(pos, transfer, weights, *halves):
    smem = pl.BlockSpec(memory_space=pltpu.SMEM)
    return pl.pallas_call(
        functools.partial(render_kernel, len(halves) - 1),
        grid=(2,),
        in_specs=[smem, smem]
        + [pl.BlockSpec((128, HALF), lambda g: (g, 0))] * len(halves)
        + [pl.BlockSpec(weights.shape, lambda g: (0, 0, 0))],
        out_specs=(
            pl.BlockSpec((128, 1024), lambda g: (g, 0)),
            pl.BlockSpec((4, 32, 8, 128), lambda g: (0, 0, 0, g)),
        ),
        scratch_shapes=[pltpu.VMEM((EDGE, 32, 8, 128), F32), pltpu.VMEM((5, 32, 8, 128), F32)],
        out_shape=(pltpu.HBM((LOCAL, 1024), jnp.int16), pltpu.HBM((4, 32, 8, LOCAL), F32)),
        compiler_params=params(semantics=("arbitrary",)),
        cost_estimate=pl.CostEstimate(flops=10**10, bytes_accessed=10**7, transcendentals=10**7),
        name="render_bricks",
    )(pos, transfer, *[in_hbm(half) for half in halves], in_hbm(weights))


def to_frame(core, sums):
    rows = iota((8, 256), 0)
    rows = jnp.where(core == 0, rows, 7 - rows)
    keep = iota((8, 256), 1) % 8 == rows
    picture = jnp.zeros((64, 128), F32)
    for tile in range(4):
        lines = []
        for c in range(4):
            for batch in range(2):
                line = jnp.where(core == 0, sums[batch][c], sums[1 - batch][c])[tile : tile + 1]
                lines.append(jnp.where(keep, line, 0.0))
        spread = ones_where(iota((256, 128), 0) // 8 + 32 * tile == iota((256, 128), 1))
        for piece in parts_of(jnp.concatenate(lines, axis=0), 3):
            picture += nn_dot(piece, spread)
    return jnp.concatenate([picture[:48], opacity(picture[48:])], axis=0).reshape(4, 16, 128)


def compose_z_kernel(pos_ref, col_ref, row_ref, first_ref, second_ref, out_ref):
    here = iota((LOCAL, LOCAL), 0)
    there = iota((LOCAL, LOCAL), 1)
    col = jnp.concatenate([col_ref[...], col_ref[...]], axis=1)
    ahead = ones_where((col < row_ref[0:1, :]) & (here % 4 == there % 4))
    group = ones_where(iota((8, LOCAL), 0) == iota((8, LOCAL), 1) % 4)
    sums = []
    for tile_ref in (first_ref, second_ref):
        depth = tile_ref[3].reshape(256, LOCAL)
        pieces = parts_of(depth, 3)
        through = jnp.exp(-sum(nn_dot(piece, ahead) for piece in pieces))
        values = [parts_of(tile_ref[c].reshape(256, LOCAL) * through, 3) for c in range(3)] + [pieces]
        sums.append([sum(nt_dot(group, piece) for piece in pieces) for pieces in values])
    out_ref[...] = to_frame(pos_ref[2], sums)


FRAME = jax.ShapeDtypeStruct((4, 16, 128), F32)


def compose_z(pos, col, row, first, second):
    return pl.pallas_call(
        compose_z_kernel,
        out_shape=FRAME,
        in_specs=[pl.BlockSpec(memory_space=pltpu.SMEM)] + [pl.BlockSpec(memory_space=pltpu.VMEM)] * 4,
        out_specs=pl.BlockSpec(memory_space=pltpu.VMEM),
        compiler_params=params(),
        cost_estimate=pl.CostEstimate(flops=10**9, bytes_accessed=4 * 10**6, transcendentals=10**5),
        name="compose_z",
    )(pos, col, row, first, second)


def compose_x_kernel(last, pos_ref, col_ref, row_ref, tile_ref, *refs):
    here = iota((LOCAL, LOCAL), 0)
    there = iota((LOCAL, LOCAL), 1)
    col = jnp.concatenate([col_ref[...], col_ref[...]], axis=1)
    ahead = ones_where((row_ref[0:1, :] < col) & (here // 4 % 4 == there // 4 % 4))
    group = ones_where(iota((8, LOCAL), 0) == iota((8, LOCAL), 1) // 4 % 4)
    codes = [tile_ref[:, c * 256 : c * 256 + 256].astype(I32).astype(F32) for c in range(4)]
    depth = jnp.exp2(codes[3] * (LOG_REACH / TOP) + LOG_MID)
    pieces = parts_of(depth, 3)
    through = jnp.exp(-sum(nn_dot(ahead, piece) for piece in pieces))
    scale = (0.5 * opacity(depth)) * through
    values = [parts_of(scale + scale * (codes[c] * (1.0 / TOP)), 3) for c in range(3)] + [pieces]
    sums = [sum(nn_dot(group, piece) for piece in pieces) for pieces in values]
    if last:
        earlier_ref, out_ref = refs
        earlier = [earlier_ref[:, c * 256 : c * 256 + 256] for c in range(4)]
        out_ref[...] = to_frame(pos_ref[2], [earlier, sums])
    else:
        (out_ref,) = refs
        for c in range(4):
            out_ref[:, c * 256 : c * 256 + 256] = sums[c]


def compose_x(pos, col, row, tiles, *earlier):
    return pl.pallas_call(
        functools.partial(compose_x_kernel, len(earlier) > 0),
        out_shape=FRAME if earlier else jax.ShapeDtypeStruct((8, 1024), F32),
        in_specs=[pl.BlockSpec(memory_space=pltpu.SMEM)]
        + [pl.BlockSpec(memory_space=pltpu.VMEM)] * (3 + len(earlier)),
        out_specs=pl.BlockSpec(memory_space=pltpu.VMEM),
        compiler_params=params(),
        cost_estimate=pl.CostEstimate(flops=10**9, bytes_accessed=10**6, transcendentals=10**5),
        name="compose_x",
    )(pos, col, row, tiles, *earlier)


def swap_cores(values):
    return lax.ppermute(values, "c", [(0, 1), (1, 0)])


def send_bricks(outbox):
    lanes = outbox.shape[1]
    sent = lax.all_to_all(outbox.reshape(CHIPS, CAP, lanes), CHIP, split_axis=0, concat_axis=0, tiled=True)
    return sent.reshape(CHIPS * CAP, lanes)


def send_tiles(tiles):
    sent = lax.all_to_all(tiles.reshape(16, 16, 1024), PLANE, split_axis=0, concat_axis=0, tiled=True)
    return sent.reshape(LOCAL, 1024)


def body(bricks, transfer, assignment, brick_cell, depth_rank):
    plane = lax.axis_index(PLANE)
    z = lax.axis_index("z")
    core = lax.axis_index("c")
    chip = plane * 4 + z

    def position(turn):
        return jnp.stack([plane, z, core, turn]).astype(I32)

    start = position(jnp.int32(-1))
    cell = brick_cell.reshape(CHIPS, LOCAL)
    cell_row = lax.dynamic_slice_in_dim(brick_cell, chip * LOCAL, LOCAL).reshape(1, LOCAL)
    major = assignment.reshape(CHIPS, LOCAL) * 16384
    key_z = major + depth_rank[0].reshape(CHIPS, LOCAL)
    key_x = major + depth_rank[1].reshape(CHIPS, LOCAL)
    weights = [plane_weights(0), plane_weights(1)]
    other = swap_cores(split_halves(start, bricks))

    inbox = send_bricks(pack(start, cell_row, bricks, other))
    place, relay_place, handing, most = index_maps(start, cell)
    keys = order_keys(start, cell, key_z, key_x)
    handing, keys = lax.optimization_barrier((handing, keys))
    cells = unpack(place, relay_place, inbox, forward(handing, inbox))

    def frames_of(cells):
        other_half = swap_cores(cells)
        tile_x, first_z = render(start, transfer, weights[0], cells)
        landed = [send_tiles(tile_x)]
        tile_x, later_z = render(start, transfer, weights[1], cells, other_half)
        landed.append(send_tiles(tile_x))
        kz_col, kz_row, kx_col, kx_row = keys
        frame_z = compose_z(start, kz_col, kz_row, first_z, later_z)
        first_x = compose_x(start, kx_col, kx_row, landed[0])
        return frame_z, compose_x(start, kx_col, kx_row, landed[1], first_x)

    def in_rounds(carry):
        rounds = (most[0] + CAP - 1) // CAP

        def next_round(carry):
            turn, cells = carry
            pos = position(turn)
            place = index_maps(pos, cell)[0]
            inbox = send_bricks(pack(pos, cell_row, bricks, other))
            return turn + 1, cells + unpack(place, relay_place, inbox, jnp.zeros((GROUP * BACK, HALF), BF16))

        nothing = (jnp.int32(0), jnp.zeros((LOCAL, HALF), BF16))
        _, cells = lax.while_loop(lambda carry: carry[0] < rounds, next_round, nothing)
        return (jnp.zeros_like(carry[0]),) + frames_of(cells)

    carry = (most[1],) + frames_of(cells)
    return lax.while_loop(lambda carry: carry[0] > 0, in_rounds, carry)[1:]


def solution(mesh):
    fine = Mesh(mesh.devices.reshape(4, 2, 2, 4, 2), CHIP + ("c",))
    in_specs = (P(CHIP + ("c",), None), P(), P(), P(), P())
    out_specs = (P(None, ("z", "c"), PLANE), P(None, ("z", "c"), PLANE))
    return jax.shard_map(body, mesh=fine, in_specs=in_specs, out_specs=out_specs, check_vma=False)
```

```python
import functools

import jax
import jax.numpy as jnp
import numpy as np
from jax import lax
from jax.experimental import pallas as pl
from jax.experimental.pallas import tpu as pltpu
from jax.sharding import Mesh
from jax.sharding import PartitionSpec as P

SIDE = 1024
EDGE = 16
CAP = 8
TRIES = 5
GROUP = 8
CLASSES = 4
BACK = 8
CHIPS = 64
LOCAL = 256
HALF = EDGE * EDGE * EDGE // 2
PIECE = 512
F32 = jnp.float32
BF16 = jnp.bfloat16
I32 = jnp.int32
LOG2E = 1.4426950408889634
KAPPA = 2.0 * 0.6931471805599453 / SIDE
PLANE = ("y", "x1", "x0")
CHIP = ("y", "x1", "x0", "z")
NEAR = ("x0", "z")


TOP = 32767.0
LOG_MID = -9.88
LOG_REACH = 9.3


def iota(shape, axis):
    return lax.broadcasted_iota(I32, shape, axis)


def ones_where(mask):
    return jnp.where(mask, 1.0, 0.0).astype(BF16)


def nt_dot(left, right):
    return lax.dot_general(left, right, (((1,), (1,)), ((), ())), preferred_element_type=F32)


def nn_dot(left, right):
    return jnp.dot(left, right, preferred_element_type=F32)


def opacity(depth):
    half = jnp.tanh(0.5 * depth)
    return 2.0 * half / (1.0 + half)


def parts_of(values, count):
    pieces = []
    rest = values
    for _ in range(count - 1):
        piece = rest.astype(BF16)
        pieces.append(piece)
        rest = rest - piece.astype(F32)
    return pieces + [rest.astype(BF16)]


def in_hbm(array):
    return pltpu.with_memory_space_constraint(array, pltpu.HBM)


def params(mib=24, semantics=None):
    return pltpu.CompilerParams(vmem_limit_bytes=mib * 1024 * 1024, dimension_semantics=semantics)


def upsample_np():
    matrix = np.zeros((2 * EDGE, EDGE), np.float32)
    for row in range(2 * EDGE):
        centre = row // 2
        beside = min(max(centre - 1 if row % 2 == 0 else centre + 1, 0), EDGE - 1)
        matrix[row, centre] += 0.75
        matrix[row, beside] += 0.25
    return matrix


def plane_weights(batch):
    up = upsample_np()
    out = np.zeros((2, 32, 8, 1 + batch, 8, 16), np.float32)
    for core in range(2):
        for sub in range(8):
            centre = 4 * batch + sub // 2
            beside = max(centre - 1, 0) if sub % 2 == 0 else centre + 1
            for m, share in ((centre, 0.75), (beside, 0.25)):
                half, y = m // 8, m % 8
                out[core, :, sub, half, y if core == 0 else 7 - y] += 0.25 * share * up
    return jnp.asarray(out.reshape(2, 256, 128 * (1 + batch)), BF16)


def chip_of(cell):
    return (cell % 64) // 4 * 4 + cell // 4096


def up(values, shift):
    inside = iota(values.shape, 1) % GROUP + shift < GROUP
    return jnp.where(inside, pltpu.roll(values, 128 - shift, axis=1), pltpu.roll(values, GROUP - shift, axis=1))


def shift_of(turn, kind):
    return 1 + (turn + 2 * kind) % (GROUP - 1)


def by_class(values, kinds, turn, back):
    out = None
    for kind in range(CLASSES):
        shift = shift_of(turn, kind)
        moved = up(values, GROUP - shift if back else shift)
        out = moved if out is None else jnp.where(kinds == kind, moved, out)
    return out


def relay_plan(counts, kinds):
    over = jnp.maximum(counts - CAP, 0.0)
    taken = jnp.minimum(counts, CAP)
    begin = jnp.zeros_like(over)
    amounts, starts, bases = [], [begin], []
    for turn in range(TRIES):
        amount = jnp.minimum(over, CAP - by_class(taken, kinds, turn, False))
        bases.append(taken)
        taken = taken + by_class(amount, kinds, turn, True)
        over = over - amount
        begin = begin + amount
        amounts.append(amount)
        starts.append(begin)
    return amounts, starts, bases, over


def plan_kernel(pos_ref, cell_ref, slot_ref):
    turn = pos_ref[3]
    kind = (pos_ref[0] * 4 + pos_ref[1]) % CLASSES
    dest = chip_of(cell_ref[...])
    across = jnp.broadcast_to(dest, (LOCAL, LOCAL))
    down = across.astype(F32).T.astype(I32)
    earlier = (down == across) & (iota((LOCAL, LOCAL), 0) < iota((LOCAL, LOCAL), 1))
    rank = jnp.sum(earlier.astype(I32), axis=0, keepdims=True)
    later = rank - turn * CAP
    in_turn = jnp.where((later >= 0) & (later < CAP), dest * CAP + later, -1)
    chips = iota((128, LOCAL), 0)
    counts = nt_dot(jnp.ones((8, LOCAL), BF16), ones_where(chips % CHIPS == dest))
    kinds = jnp.full((8, 128), kind, I32)
    _, starts, bases, _ = relay_plan(counts, kinds)
    rows = starts[1:] + [by_class(base, kinds, n, False) for n, base in enumerate(bases)]
    table = jnp.concatenate([row[0:1] for row in rows] + [jnp.zeros((16 - len(rows), 128), F32)], axis=0)
    found = nn_dot(table.astype(BF16), ones_where(chips == dest)).astype(I32)
    relayed = jnp.where(rank < CAP, dest * CAP + rank, -1)
    over = rank - CAP
    for n in range(TRIES):
        begin = found[n - 1 : n] if n else jnp.zeros_like(over)
        inside = (over >= begin) & (over < found[n : n + 1])
        relay = dest // GROUP * GROUP + (dest + shift_of(n, kind)) % GROUP
        relayed = jnp.where(inside, relay * CAP + found[TRIES + n : TRIES + n + 1] + over - begin, relayed)
    slot_ref[...] = jnp.where(turn < 0, relayed, in_turn)


def plan_slots(pos, cell_row):
    return pl.pallas_call(
        plan_kernel,
        out_shape=jax.ShapeDtypeStruct((1, LOCAL), I32),
        in_specs=[pl.BlockSpec(memory_space=pltpu.SMEM), pl.BlockSpec(memory_space=pltpu.VMEM)],
        out_specs=pl.BlockSpec(memory_space=pltpu.VMEM),
        compiler_params=params(),
        cost_estimate=pl.CostEstimate(flops=10**9, bytes_accessed=10**6, transcendentals=0),
        name="plan_slots",
    )(pos, cell_row)


def pack_kernel(pos_ref, slot_ref, bricks_ref, other_ref, out_ref, full_ref, box_ref, sems):
    core = pos_ref[2]
    slot = slot_ref[...]
    for n, ref in enumerate((bricks_ref, other_ref)):
        rows = pl.ds(pl.multiple_of((core + n) % 2 * 128, 128), 128)
        for x in range(EDGE):
            start = pl.multiple_of(x * 256 + core * 128, 128)
            full_ref[rows, x * 128 : x * 128 + 128] = ref[:, pl.ds(start, 128)]
    pick = ones_where(iota((CHIPS * CAP, LOCAL), 0) == slot)
    copies = []
    for at in range(HALF // PIECE):
        lanes = pl.ds(at * PIECE, PIECE)
        box_ref[:, lanes] = nn_dot(pick, full_ref[:, lanes]).astype(BF16)
        copy = pltpu.make_async_copy(box_ref.at[:, lanes], out_ref.at[:, lanes], sems.at[at])
        copy.start()
        copies.append(copy)
    for copy in copies:
        copy.wait()


def pack(pos, slot, bricks, other):
    rows = CHIPS * CAP
    return pl.pallas_call(
        pack_kernel,
        in_specs=[pl.BlockSpec(memory_space=pltpu.SMEM)] + [pl.BlockSpec(memory_space=pltpu.VMEM)] * 3,
        out_specs=pl.BlockSpec(memory_space=pltpu.HBM),
        scratch_shapes=[
            pltpu.VMEM((LOCAL, HALF), BF16),
            pltpu.VMEM((rows, HALF), BF16),
            pltpu.SemaphoreType.DMA((HALF // PIECE,)),
        ],
        out_shape=pltpu.HBM((rows, HALF), BF16),
        compiler_params=params(),
        name="pack_outbox",
    )(pos, slot, bricks, other)


def index_kernel(
    pos_ref, cell_ref, place_ref, relay_place_ref, forward_ref, most_ref, left_ref,
    here_ref, slot_ref, relay_ref, dest_ref, count_ref, side_ref
):
    plane, z, turn = pos_ref[0], pos_ref[1], pos_ref[3]
    me = plane * 4 + z
    mine = me % GROUP
    first = me - mine
    cell = cell_ref[...]
    gx, gz = cell % 64, cell // 64 % 64
    dest = chip_of(cell)
    dest_ref[...] = dest
    down_128 = iota((128, LOCAL), 0)
    down_chip = down_128 % CHIPS
    units = jnp.ones((8, LOCAL), BF16)

    def count(index, carry):
        row = pl.ds(index, 1)
        count_ref[row, :] = nt_dot(units, ones_where(down_chip == dest_ref[row, :]))[0:1]
        return carry

    lax.fori_loop(0, CHIPS, count, 0, unroll=8)
    counts = count_ref[...]
    most_ref[0] = jnp.max(counts).astype(I32)
    kinds = iota((CHIPS, 128), 0) % CLASSES
    amounts, starts, bases, left = relay_plan(counts, kinds)
    sources = ones_where(iota((CHIPS, CHIPS), 1) < iota((CHIPS, CHIPS), 0))
    lane = iota((CHIPS, 128), 1)

    def column(values, chip):
        return jnp.sum(jnp.where(lane == chip, values, 0.0), axis=1, keepdims=True)

    for_me = dest == me
    before = ones_where(iota((LOCAL, LOCAL), 0) < iota((LOCAL, LOCAL), 1))
    rank = nn_dot(ones_where(for_me), before).astype(I32)
    over = rank - CAP
    slots = CHIPS * CAP
    spread = jnp.where(iota((CHIPS, slots), 1) // CAP == iota((CHIPS, slots), 0), 1.0, 0.0)
    along = lambda col: jnp.sum(col * spread, axis=0, keepdims=True).astype(I32)
    slot_lane = iota((1, slots), 1) % CAP
    relay = jnp.full((CHIPS, LOCAL), -1, I32)
    handed = jnp.full((1, slots), -1, I32)
    for shift in range(1, GROUP):
        amount = jnp.zeros((CHIPS, 128), F32)
        begin = amount
        base = amount
        for kind in range(CLASSES):
            for n in range(TRIES):
                if shift_of(n, kind) == shift:
                    amount = jnp.where(kinds == kind, amounts[n], amount)
                    begin = jnp.where(kinds == kind, starts[n], begin)
                    base = jnp.where(kinds == kind, bases[n], base)
        prefix = nn_dot(sources, amount.astype(BF16))
        left = left + jnp.maximum(jnp.sum(amount, axis=0, keepdims=True) - BACK, 0.0)
        order = over - column(begin, me).astype(I32)
        at = (mine + shift) % GROUP * BACK + column(prefix, me).astype(I32) + order
        relay = jnp.where((order >= 0) & (order < column(amount, me).astype(I32)), at, relay)
        near = (mine + GROUP - shift) % GROUP
        order = slot_lane - along(column(base, me))
        at = near * BACK + order + along(column(prefix, first + near))
        handed = jnp.where((order >= 0) & (order < along(column(amount, first + near))), at, handed)
    forward_ref[...] = ones_where(iota((GROUP * BACK, slots), 0) == handed)
    left_ref[0] = jnp.max(left).astype(I32)
    relay_ref[...] = jnp.where(for_me & (turn < 0), relay, -1)
    group = iota((CHIPS, LOCAL), 0) % (128 // CAP)
    later = rank - jnp.maximum(turn, 0) * CAP
    slot_ref[...] = jnp.where(for_me & (later >= 0) & (later < CAP), later + group * CAP, -1)
    here_ref[...] = jnp.where(for_me, gz * 4 + gx % 4, -1)
    down_256 = iota((LOCAL, LOCAL), 0)
    side_ref[...] = jnp.zeros((LOCAL, 128), F32)
    for part in range(slots // 128):

        def source(index, place):
            row = pl.ds(part * (128 // CAP) + index, 1)
            here = ones_where(down_256 == here_ref[row, :])
            wanted = jnp.concatenate(
                [ones_where(down_128 == slot_ref[row, :]), ones_where(down_128 == relay_ref[row, :])], axis=0
            )
            both = nt_dot(here, wanted)
            side_ref[...] += both[:, 128:]
            return place + both[:, :128]

        place = lax.fori_loop(0, 128 // CAP, source, jnp.zeros((LOCAL, 128), F32), unroll=4)
        place_ref[:, part * 128 : part * 128 + 128] = place.astype(BF16)
    relay_place_ref[...] = side_ref[...].astype(BF16)


def index_maps(pos, cell):
    vmem = pl.BlockSpec(memory_space=pltpu.VMEM)
    return pl.pallas_call(
        index_kernel,
        out_shape=(
            pltpu.HBM((LOCAL, CHIPS * CAP), BF16),
            pltpu.HBM((LOCAL, 128), BF16),
            jax.ShapeDtypeStruct((GROUP * BACK, CHIPS * CAP), BF16),
            jax.ShapeDtypeStruct((1,), I32),
            jax.ShapeDtypeStruct((1,), I32),
        ),
        in_specs=[pl.BlockSpec(memory_space=pltpu.SMEM), vmem],
        grid=(1,),
        out_specs=(
            pl.BlockSpec((LOCAL, CHIPS * CAP), lambda s: (0, 0)),
            pl.BlockSpec((LOCAL, 128), lambda s: (0, 0)),
            pl.BlockSpec((GROUP * BACK, CHIPS * CAP), lambda s: (0, 0)),
            pl.BlockSpec(memory_space=pltpu.SMEM),
            pl.BlockSpec(memory_space=pltpu.SMEM),
        ),
        scratch_shapes=[pltpu.VMEM((CHIPS, LOCAL), I32)] * 4
        + [pltpu.VMEM((CHIPS, 128), F32), pltpu.VMEM((LOCAL, 128), F32)],
        compiler_params=params(),
        cost_estimate=pl.CostEstimate(flops=10**10, bytes_accessed=10**6, transcendentals=0),
        name="index_maps",
    )(pos, cell)


def key_kernel(pos_ref, cell_ref, key_z_ref, key_x_ref, ahead_z_ref, ahead_x_ref, here_ref, there_ref):
    plane, z = pos_ref[0], pos_ref[1]
    cell = cell_ref[...]
    gx, gz, gy = cell % 64, cell // 64 % 64, cell // 4096
    here_ref[...] = jnp.where((gy == z) & (gx // 4 == plane), gz * 4 + gx % 4, -1)
    there_ref[...] = jnp.where((gy == z) & (gz // 4 == plane), gx // 4 * 16 + gz % 4 * 4 + gx % 4, -1)
    down = iota((LOCAL, LOCAL), 0)
    byte = iota((8, LOCAL), 0)

    def key_bytes(row):
        return jnp.where(
            byte == 0, row % 256, jnp.where(byte == 1, row // 256 % 256, jnp.where(byte == 2, row // 65536, 0))
        ).astype(F32).astype(BF16)

    def source(index, sums):
        row = pl.ds(index, 1)
        return (
            sums[0] + nt_dot(ones_where(down == here_ref[row, :]), key_bytes(key_z_ref[row, :])),
            sums[1] + nt_dot(ones_where(down == there_ref[row, :]), key_bytes(key_x_ref[row, :])),
        )

    nothing = jnp.zeros((LOCAL, 8), F32)
    sums = lax.fori_loop(0, CHIPS, source, (nothing, nothing), unroll=4)
    across = iota((LOCAL, LOCAL), 1)

    def key_of(part):
        return jnp.broadcast_to(part[:, 0:1] + 256.0 * part[:, 1:2] + 65536.0 * part[:, 2:3], (LOCAL, LOCAL))

    key_z, key_x = key_of(sums[0]), key_of(sums[1])
    ahead_z_ref[...] = ones_where((key_z < key_z.T) & (down % 4 == across % 4))
    ahead_x_ref[...] = ones_where((key_x.T < key_x) & (down // 4 % 4 == across // 4 % 4))


def order_keys(pos, cell, key_z, key_x):
    vmem = pl.BlockSpec(memory_space=pltpu.VMEM)
    ahead = jax.ShapeDtypeStruct((LOCAL, LOCAL), BF16)
    return pl.pallas_call(
        key_kernel,
        out_shape=(ahead, ahead),
        in_specs=[pl.BlockSpec(memory_space=pltpu.SMEM), vmem, vmem, vmem],
        out_specs=(vmem,) * 2,
        scratch_shapes=[pltpu.VMEM((CHIPS, LOCAL), I32)] * 2,
        compiler_params=params(),
        cost_estimate=pl.CostEstimate(flops=10**10, bytes_accessed=10**6, transcendentals=0),
        name="order_keys",
    )(pos, cell, key_z, key_x)


def forward_kernel(forward_ref, recv_ref, out_ref):
    out_ref[...] = nn_dot(forward_ref[...], recv_ref[...]).astype(BF16)


def forward(maps, received):
    vmem = pl.BlockSpec(memory_space=pltpu.VMEM)
    handed = pl.pallas_call(
        forward_kernel,
        out_shape=jax.ShapeDtypeStruct((GROUP * BACK, HALF), BF16),
        in_specs=[vmem, vmem],
        out_specs=vmem,
        compiler_params=params(),
        cost_estimate=pl.CostEstimate(flops=10**8, bytes_accessed=10**6, transcendentals=0),
        name="hand_on",
    )(maps, received)
    sent = lax.all_to_all(handed.reshape(GROUP, BACK, HALF), NEAR, split_axis=0, concat_axis=0, tiled=True)
    return sent.reshape(GROUP * BACK, HALF)


def unpack_kernel(place_ref, relay_ref, recv_ref, back_ref, out_ref, cells_ref, sems):
    copies = []
    for at in range(HALF // PIECE):
        lanes = pl.ds(at * PIECE, PIECE)
        cells = nn_dot(place_ref[...], recv_ref[:, lanes]) + nn_dot(relay_ref[:, : GROUP * BACK], back_ref[:, lanes])
        cells_ref[:, lanes] = cells.astype(BF16)
        copies.append(pltpu.make_async_copy(cells_ref.at[:, lanes], out_ref.at[:, lanes], sems.at[at]))
        copies[-1].start()
    for copy in copies:
        copy.wait()


def unpack(place, relay_place, received, back):
    vmem = pl.BlockSpec(memory_space=pltpu.VMEM)
    return pl.pallas_call(
        unpack_kernel,
        out_shape=pltpu.HBM((LOCAL, HALF), BF16),
        in_specs=[vmem] * 4,
        out_specs=pl.BlockSpec(memory_space=pltpu.HBM),
        scratch_shapes=[pltpu.VMEM((LOCAL, HALF), BF16), pltpu.SemaphoreType.DMA((HALF // PIECE,))],
        compiler_params=params(),
        cost_estimate=pl.CostEstimate(flops=10**9, bytes_accessed=3 * 10**6, transcendentals=0),
        name="unpack_inbox",
    )(place, relay_place, received, back)


def render_group(views, pos_ref, transfer_ref, halves, weights_ref, tile_x_ref, tile_z_ref, plane_ref, state_ref):
    with_x, with_z = "x" in views, "z" in views

    for x in range(EDGE):
        operand = jnp.concatenate([ref[:, x * 128 : x * 128 + 128] for ref in halves], axis=1)
        plane_ref[x] = nt_dot(weights_ref[pos_ref[2]], operand).reshape(32, 8, 128)
    slope = [transfer_ref[0, 0] * LOG2E] + [0.5 * transfer_ref[0, c] for c in (1, 2, 3)]
    offset = [transfer_ref[1, 0] * LOG2E] + [0.5 * transfer_ref[1, c] for c in (1, 2, 3)]
    zero = jnp.zeros((8, 128), F32)
    one = jnp.ones((8, 128), F32)
    if with_x:
        state_ref[0] = jnp.ones((32, 8, 128), F32)
        for n in range(1, 5):
            state_ref[n] = jnp.zeros((32, 8, 128), F32)

    def classify(sample):
        grown = jnp.exp2(slope[0] * sample + offset[0])
        above = 1.0 + grown
        dense = jnp.log2(above) * (grown * pl.reciprocal(above - 1.0, approx=True))
        alpha = dense * (KAPPA - dense * (KAPPA * KAPPA / 2 - dense * (KAPPA * KAPPA * KAPPA / 6)))
        return dense, alpha, [jnp.tanh(slope[c] * sample + offset[c]) for c in (1, 2, 3)]

    def advance(state, values):
        dense, alpha, colours = values
        weight = alpha * state[0]
        return (
            state[0] - weight,
            state[1] + colours[0] * weight,
            state[2] + colours[1] * weight,
            state[3] + colours[2] * weight,
            state[4] + dense,
        )

    def result(state):
        depth = KAPPA * state[4]
        half = 0.5 * opacity(depth)
        return [half + 0.5 * state[1], half + 0.5 * state[2], half + 0.5 * state[3], depth]

    def coded(state):
        depth = KAPPA * state[4]
        scale = TOP / opacity(depth)
        codes = [jnp.floor(scale * state[c] + 0.5) for c in (1, 2, 3)]
        codes.append(jnp.floor((jnp.log2(depth) - LOG_MID) * (TOP / LOG_REACH) + 0.5))
        return [jnp.clip(code, -TOP, TOP) for code in codes]

    def slab(x, carry):
        left = jnp.maximum(x - 1, 0)
        right = jnp.minimum(x + 1, EDGE - 1)

        def columns(view_even, view_odd):
            for k in range(32):
                centre = 3.0 * plane_ref[x, k]
                even = classify(centre + plane_ref[left, k])
                odd = classify(centre + plane_ref[right, k])
                if with_z:
                    view_even = advance(view_even, even)
                    view_odd = advance(view_odd, odd)
                if with_x:
                    state = tuple(state_ref[n, k] for n in range(5))
                    state = advance(advance(state, even), odd)
                    for n in range(5):
                        state_ref[n, k] = state[n]
            return view_even, view_odd

        start = (one, zero, zero, zero, zero)
        pixels = columns(start, start)
        for odd in range(2 if with_z else 0):
            values = result(pixels[odd])
            for c in range(4):
                tile_z_ref[c, 2 * x + odd] = values[c]
        return carry

    lax.fori_loop(0, EDGE, slab, 0)
    if with_x:
        values = coded([state_ref[n] for n in range(5)])
        for c in range(4):
            tile_x_ref[:, c * 256 : c * 256 + 256] = values[c].reshape(256, 128).T.astype(I32).astype(jnp.int16)


def render_kernel(views, count, pos_ref, transfer_ref, *refs):
    halves, weights_ref, rest = refs[:count], refs[count], list(refs[count + 1 :])
    tile_x_ref = rest.pop(0) if "x" in views[0] else None
    tile_z_ref, plane_ref, state_ref = rest
    for g, wanted in enumerate(views):
        if len(set(views)) == 1:
            if g == 0:
                render_group(wanted, pos_ref, transfer_ref, halves, weights_ref, tile_x_ref, tile_z_ref, plane_ref, state_ref)
        else:

            @pl.when(pl.program_id(0) == g)
            def _():
                render_group(wanted, pos_ref, transfer_ref, halves, weights_ref, tile_x_ref, tile_z_ref, plane_ref, state_ref)


def render(views, first, pos, transfer, weights, *halves):
    smem = pl.BlockSpec(memory_space=pltpu.SMEM)
    groups_z = sum("z" in wanted for wanted in views)
    out_specs = [pl.BlockSpec((4, 32, 8, 128), lambda g: (0, 0, 0, jnp.minimum(g, groups_z - 1)))]
    out_shape = [pltpu.HBM((4, 32, 8, 128 * groups_z), F32)]
    if "x" in views[0]:
        out_specs.insert(0, pl.BlockSpec((128, 1024), lambda g: (g, 0)))
        out_shape.insert(0, pltpu.HBM((128 * len(views), 1024), jnp.int16))
    return pl.pallas_call(
        functools.partial(render_kernel, views, len(halves)),
        grid=(len(views),),
        in_specs=[smem, smem]
        + [pl.BlockSpec((128, HALF), lambda g: (g + first, 0))] * len(halves)
        + [pl.BlockSpec(weights.shape, lambda g: (0, 0, 0))],
        out_specs=out_specs,
        scratch_shapes=[pltpu.VMEM((EDGE, 32, 8, 128), F32), pltpu.VMEM((5, 32, 8, 128), F32)],
        out_shape=out_shape,
        compiler_params=params(semantics=("arbitrary",)),
        cost_estimate=pl.CostEstimate(flops=10**10, bytes_accessed=10**7, transcendentals=10**7),
        name="render_" + "_".join(views),
    )(pos, transfer, in_hbm(halves[0]), *halves[1:], weights)


def to_frame(core, sums):
    rows = iota((8, 256), 0)
    rows = jnp.where(core == 0, rows, 7 - rows)
    keep = iota((8, 256), 1) % 8 == rows
    picture = jnp.zeros((64, 128), F32)
    for tile in range(4):
        lines = []
        for c in range(4):
            for batch in range(2):
                line = jnp.where(core == 0, sums[batch][c], sums[1 - batch][c])[tile : tile + 1]
                lines.append(jnp.where(keep, line, 0.0))
        spread = ones_where(iota((256, 128), 0) // 8 + 32 * tile == iota((256, 128), 1))
        stacked = nn_dot(jnp.concatenate(parts_of(jnp.concatenate(lines, axis=0), 3), axis=0), spread)
        picture += stacked[:64] + stacked[64:128] + stacked[128:]
    return jnp.concatenate([picture[:48], opacity(picture[48:])], axis=0).reshape(4, 16, 128)


def compose_z_kernel(pos_ref, ahead_ref, first_ref, second_ref, third_ref, out_ref):
    ahead = ahead_ref[...]
    group = ones_where(iota((8, LOCAL), 0) == iota((8, LOCAL), 1) % 4)
    sums = []
    first = [first_ref[c] for c in range(4)]
    second = [jnp.concatenate([second_ref[c], third_ref[c]], axis=2) for c in range(4)]
    for tile in (first, second):
        depth = tile[3].reshape(256, LOCAL)
        pieces = parts_of(depth, 3)
        through = jnp.exp(-sum(nn_dot(piece, ahead) for piece in pieces))
        values = [parts_of(tile[c].reshape(256, LOCAL) * through, 3) for c in range(3)] + [pieces]
        sums.append([sum(nt_dot(group, piece) for piece in pieces) for pieces in values])
    out_ref[...] = to_frame(pos_ref[2], sums)


FRAME = jax.ShapeDtypeStruct((4, 16, 128), F32)


def compose_z(pos, ahead, *tiles):
    return pl.pallas_call(
        compose_z_kernel,
        out_shape=FRAME,
        in_specs=[pl.BlockSpec(memory_space=pltpu.SMEM)] + [pl.BlockSpec(memory_space=pltpu.VMEM)] * 4,
        out_specs=pl.BlockSpec(memory_space=pltpu.VMEM),
        compiler_params=params(),
        cost_estimate=pl.CostEstimate(flops=10**9, bytes_accessed=4 * 10**6, transcendentals=10**5),
        name="compose_z",
    )(pos, ahead, *tiles)


def compose_x_kernel(last, pos_ref, ahead_ref, tile_ref, *refs):
    ahead = ahead_ref[...]
    codes = [tile_ref[:, c * 256 : c * 256 + 256].astype(I32).astype(F32) for c in range(4)]
    depth = jnp.exp2(codes[3] * (LOG_REACH / TOP) + LOG_MID)
    pieces = parts_of(depth, 3)
    through = jnp.exp(-sum(nn_dot(ahead, piece) for piece in pieces))
    scale = (0.5 * opacity(depth)) * through
    values = [scale + scale * (codes[c] * (1.0 / TOP)) for c in range(3)] + [depth]
    group = ones_where(iota((8, 48), 0) == iota((8, 48), 1) % 16 // 4)
    folded = [jnp.sum(value.reshape(16, 16, 256), axis=0) for value in values]
    sums = [nn_dot(group, jnp.concatenate(parts_of(fold, 3), axis=0)) for fold in folded]
    if last:
        earlier_ref, out_ref = refs
        earlier = [earlier_ref[:, c * 256 : c * 256 + 256] for c in range(4)]
        out_ref[...] = to_frame(pos_ref[2], [earlier, sums])
    else:
        (out_ref,) = refs
        for c in range(4):
            out_ref[:, c * 256 : c * 256 + 256] = sums[c]


def compose_x(pos, ahead, tiles, *earlier):
    return pl.pallas_call(
        functools.partial(compose_x_kernel, len(earlier) > 0),
        out_shape=FRAME if earlier else jax.ShapeDtypeStruct((8, 1024), F32),
        in_specs=[pl.BlockSpec(memory_space=pltpu.SMEM)]
        + [pl.BlockSpec(memory_space=pltpu.VMEM)] * (2 + len(earlier)),
        out_specs=pl.BlockSpec(memory_space=pltpu.VMEM),
        compiler_params=params(),
        cost_estimate=pl.CostEstimate(flops=10**9, bytes_accessed=10**6, transcendentals=10**5),
        name="compose_x",
    )(pos, ahead, tiles, *earlier)


def swap_cores(values):
    return lax.ppermute(values, "c", [(0, 1), (1, 0)])


def send_bricks(outbox):
    lanes = outbox.shape[1]
    sent = lax.all_to_all(outbox.reshape(CHIPS, CAP, lanes), CHIP, split_axis=0, concat_axis=0, tiled=True)
    return sent.reshape(CHIPS * CAP, lanes)


def send_tiles(tiles):
    sent = lax.all_to_all(tiles.reshape(16, 16, 1024), PLANE, split_axis=0, concat_axis=0, tiled=True)
    return sent.reshape(LOCAL, 1024)


def body(bricks, transfer, assignment, brick_cell, depth_rank):
    plane = lax.axis_index(PLANE)
    z = lax.axis_index("z")
    core = lax.axis_index("c")
    chip = plane * 4 + z

    def position(turn):
        return jnp.stack([plane, z, core, turn]).astype(I32)

    start = position(jnp.int32(-1))
    cell_row = lax.dynamic_slice_in_dim(brick_cell, chip * LOCAL, LOCAL).reshape(1, LOCAL)
    weights = [plane_weights(0), plane_weights(1)]
    other = swap_cores(bricks)

    outbox = pack(start, plan_slots(start, cell_row), bricks, other)
    outbox, brick_cell, assignment, depth_rank = lax.optimization_barrier((outbox, brick_cell, assignment, depth_rank))
    inbox = send_bricks(outbox)
    cell = brick_cell.reshape(CHIPS, LOCAL)
    major = assignment.reshape(CHIPS, LOCAL) * 16384
    key_z = major + depth_rank[0].reshape(CHIPS, LOCAL)
    key_x = major + depth_rank[1].reshape(CHIPS, LOCAL)
    place, relay_place, handing, most, left = index_maps(start, cell)
    keys = order_keys(start, cell, key_z, key_x)
    handing, keys = lax.optimization_barrier((handing, keys))
    cells = unpack(place, relay_place, inbox, forward(handing, inbox))

    def frames_of(cells):
        other_half = swap_cores(cells)
        tile_x, first_z = render(("xz", "xz"), 0, start, transfer, weights[0], cells)
        landed = [send_tiles(tile_x)]
        tile_x, near_z = render(("xz", "x"), 0, start, transfer, weights[1], cells, other_half)
        cells, tile_x, landed[0] = lax.optimization_barrier((cells, tile_x, landed[0]))
        landed.append(send_tiles(tile_x))
        (far_z,) = render(("z",), 1, start, transfer, weights[1], cells, other_half)
        ahead_z, ahead_x = keys
        frame_z = compose_z(start, ahead_z, first_z, near_z, far_z)
        first_x = compose_x(start, ahead_x, landed[0])
        return frame_z, compose_x(start, ahead_x, landed[1], first_x)

    def in_rounds(carry):
        rounds = (most.reshape(()) + CAP - 1) // CAP

        def next_round(carry):
            turn, cells = carry
            pos = position(turn)
            place = index_maps(pos, cell)[0]
            inbox = send_bricks(pack(pos, plan_slots(pos, cell_row), bricks, other))
            return turn + 1, cells + unpack(place, relay_place, inbox, jnp.zeros((GROUP * BACK, HALF), BF16))

        nothing = (jnp.int32(0), jnp.zeros((LOCAL, HALF), BF16))
        _, cells = lax.while_loop(lambda carry: carry[0] < rounds, next_round, nothing)
        return (jnp.zeros_like(carry[0]),) + frames_of(cells)

    carry = (left.reshape(()),) + frames_of(cells)
    return lax.while_loop(lambda carry: carry[0] > 0, in_rounds, carry)[1:]


def solution(mesh):
    fine = Mesh(mesh.devices.reshape(4, 2, 2, 4, 2), CHIP + ("c",))
    in_specs = (P(CHIP + ("c",), None), P(), P(), P(), P())
    out_specs = (P(None, ("z", "c"), PLANE), P(None, ("z", "c"), PLANE))
    return jax.shard_map(body, mesh=fine, in_specs=in_specs, out_specs=out_specs, check_vma=False)
```

```python
import functools

import jax
import jax.numpy as jnp
import numpy as np
from jax import lax
from jax.experimental import pallas as pl
from jax.experimental.pallas import tpu as pltpu
from jax.sharding import Mesh
from jax.sharding import PartitionSpec as P

SIDE = 1024
EDGE = 16
CAP = 8
TRIES = 5
GROUP = 8
CLASSES = 4
BACK = 8
CHIPS = 64
LOCAL = 256
HALF = EDGE * EDGE * EDGE // 2
PIECE = 512
F32 = jnp.float32
BF16 = jnp.bfloat16
I32 = jnp.int32
LOG2E = 1.4426950408889634
KAPPA = 2.0 * 0.6931471805599453 / SIDE
PLANE = ("y", "x1", "x0")
CHIP = ("y", "x1", "x0", "z")
NEAR = ("x0", "z")


TOP = 32767.0
LOG_MID = -9.88
LOG_REACH = 9.3


def iota(shape, axis):
    return lax.broadcasted_iota(I32, shape, axis)


def ones_where(mask):
    return jnp.where(mask, 1.0, 0.0).astype(BF16)


def nt_dot(left, right):
    return lax.dot_general(left, right, (((1,), (1,)), ((), ())), preferred_element_type=F32)


def nn_dot(left, right):
    return jnp.dot(left, right, preferred_element_type=F32)


def opacity(depth):
    half = jnp.tanh(0.5 * depth)
    return 2.0 * half / (1.0 + half)


def parts_of(values, count):
    pieces = []
    rest = values
    for _ in range(count - 1):
        piece = rest.astype(BF16)
        pieces.append(piece)
        rest = rest - piece.astype(F32)
    return pieces + [rest.astype(BF16)]


def in_hbm(array):
    return pltpu.with_memory_space_constraint(array, pltpu.HBM)


def params(mib=24, semantics=None):
    return pltpu.CompilerParams(vmem_limit_bytes=mib * 1024 * 1024, dimension_semantics=semantics)


def upsample_np():
    matrix = np.zeros((2 * EDGE, EDGE), np.float32)
    for row in range(2 * EDGE):
        centre = row // 2
        beside = min(max(centre - 1 if row % 2 == 0 else centre + 1, 0), EDGE - 1)
        matrix[row, centre] += 0.75
        matrix[row, beside] += 0.25
    return matrix


def plane_weights(batch):
    up = upsample_np()
    out = np.zeros((2, 32, 8, 1 + batch, 8, 16), np.float32)
    for core in range(2):
        for sub in range(8):
            centre = 4 * batch + sub // 2
            beside = max(centre - 1, 0) if sub % 2 == 0 else centre + 1
            for m, share in ((centre, 0.75), (beside, 0.25)):
                half, y = m // 8, m % 8
                out[core, :, sub, half, y if core == 0 else 7 - y] += 0.25 * share * up
    return jnp.asarray(out.reshape(2, 256, 128 * (1 + batch)), BF16)


def chip_of(cell):
    return (cell % 64) // 4 * 4 + cell // 4096


def up(values, shift):
    inside = iota(values.shape, 1) % GROUP + shift < GROUP
    return jnp.where(inside, pltpu.roll(values, 128 - shift, axis=1), pltpu.roll(values, GROUP - shift, axis=1))


def shift_of(turn, kind):
    return 1 + (turn + 2 * kind) % (GROUP - 1)


def by_class(values, kinds, turn, back):
    out = None
    for kind in range(CLASSES):
        shift = shift_of(turn, kind)
        moved = up(values, GROUP - shift if back else shift)
        out = moved if out is None else jnp.where(kinds == kind, moved, out)
    return out


def relay_plan(counts, kinds):
    over = jnp.maximum(counts - CAP, 0.0)
    taken = jnp.minimum(counts, CAP)
    begin = jnp.zeros_like(over)
    amounts, starts, bases = [], [begin], []
    for turn in range(TRIES):
        amount = jnp.minimum(over, CAP - by_class(taken, kinds, turn, False))
        bases.append(taken)
        taken = taken + by_class(amount, kinds, turn, True)
        over = over - amount
        begin = begin + amount
        amounts.append(amount)
        starts.append(begin)
    return amounts, starts, bases, over


def plan_kernel(pos_ref, cell_ref, slot_ref):
    turn = pos_ref[3]
    kind = (pos_ref[0] * 4 + pos_ref[1]) % CLASSES
    dest = chip_of(cell_ref[...])
    across = jnp.broadcast_to(dest, (LOCAL, LOCAL))
    down = across.astype(F32).T.astype(I32)
    earlier = (down == across) & (iota((LOCAL, LOCAL), 0) < iota((LOCAL, LOCAL), 1))
    rank = jnp.sum(earlier.astype(I32), axis=0, keepdims=True)
    later = rank - turn * CAP
    in_turn = jnp.where((later >= 0) & (later < CAP), dest * CAP + later, -1)
    chips = iota((128, LOCAL), 0)
    counts = nt_dot(jnp.ones((8, LOCAL), BF16), ones_where(chips % CHIPS == dest))
    kinds = jnp.full((8, 128), kind, I32)
    _, starts, bases, _ = relay_plan(counts, kinds)
    rows = starts[1:] + [by_class(base, kinds, n, False) for n, base in enumerate(bases)]
    table = jnp.concatenate([row[0:1] for row in rows] + [jnp.zeros((16 - len(rows), 128), F32)], axis=0)
    found = nn_dot(table.astype(BF16), ones_where(chips == dest)).astype(I32)
    relayed = jnp.where(rank < CAP, dest * CAP + rank, -1)
    over = rank - CAP
    for n in range(TRIES):
        begin = found[n - 1 : n] if n else jnp.zeros_like(over)
        inside = (over >= begin) & (over < found[n : n + 1])
        relay = dest // GROUP * GROUP + (dest + shift_of(n, kind)) % GROUP
        relayed = jnp.where(inside, relay * CAP + found[TRIES + n : TRIES + n + 1] + over - begin, relayed)
    slot_ref[...] = jnp.where(turn < 0, relayed, in_turn)


def plan_slots(pos, cell_row):
    return pl.pallas_call(
        plan_kernel,
        out_shape=jax.ShapeDtypeStruct((1, LOCAL), I32),
        in_specs=[pl.BlockSpec(memory_space=pltpu.SMEM), pl.BlockSpec(memory_space=pltpu.VMEM)],
        out_specs=pl.BlockSpec(memory_space=pltpu.VMEM),
        compiler_params=params(),
        cost_estimate=pl.CostEstimate(flops=10**9, bytes_accessed=10**6, transcendentals=0),
        name="plan_slots",
    )(pos, cell_row)


def pack_kernel(pos_ref, slot_ref, bricks_ref, other_ref, out_ref, full_ref, box_ref, sems):
    core = pos_ref[2]
    slot = slot_ref[...]
    for n, ref in enumerate((bricks_ref, other_ref)):
        rows = pl.ds(pl.multiple_of((core + n) % 2 * 128, 128), 128)
        for x in range(EDGE):
            start = pl.multiple_of(x * 256 + core * 128, 128)
            full_ref[rows, x * 128 : x * 128 + 128] = ref[:, pl.ds(start, 128)]
    pick = ones_where(iota((CHIPS * CAP, LOCAL), 0) == slot)
    copies = []
    for at in range(HALF // PIECE):
        lanes = pl.ds(at * PIECE, PIECE)
        box_ref[:, lanes] = nn_dot(pick, full_ref[:, lanes]).astype(BF16)
        copy = pltpu.make_async_copy(box_ref.at[:, lanes], out_ref.at[:, lanes], sems.at[at])
        copy.start()
        copies.append(copy)
    for copy in copies:
        copy.wait()


def pack(pos, slot, bricks, other):
    rows = CHIPS * CAP
    return pl.pallas_call(
        pack_kernel,
        in_specs=[pl.BlockSpec(memory_space=pltpu.SMEM)] + [pl.BlockSpec(memory_space=pltpu.VMEM)] * 3,
        out_specs=pl.BlockSpec(memory_space=pltpu.HBM),
        scratch_shapes=[
            pltpu.VMEM((LOCAL, HALF), BF16),
            pltpu.VMEM((rows, HALF), BF16),
            pltpu.SemaphoreType.DMA((HALF // PIECE,)),
        ],
        out_shape=pltpu.HBM((rows, HALF), BF16),
        compiler_params=params(),
        name="pack_outbox",
    )(pos, slot, bricks, other)


def index_kernel(
    pos_ref, cell_ref, place_ref, relay_place_ref, forward_ref, most_ref, left_ref,
    here_ref, slot_ref, relay_ref, dest_ref, count_ref, side_ref
):
    plane, z, turn = pos_ref[0], pos_ref[1], pos_ref[3]
    me = plane * 4 + z
    mine = me % GROUP
    first = me - mine
    cell = cell_ref[...]
    gx, gz = cell % 64, cell // 64 % 64
    dest = chip_of(cell)
    dest_ref[...] = dest
    down_128 = iota((128, LOCAL), 0)
    down_chip = down_128 % CHIPS
    units = jnp.ones((8, LOCAL), BF16)

    def count(index, carry):
        row = pl.ds(index, 1)
        count_ref[row, :] = nt_dot(units, ones_where(down_chip == dest_ref[row, :]))[0:1]
        return carry

    lax.fori_loop(0, CHIPS, count, 0, unroll=8)
    counts = count_ref[...]
    most_ref[0] = jnp.max(counts).astype(I32)
    kinds = iota((CHIPS, 128), 0) % CLASSES
    amounts, starts, bases, left = relay_plan(counts, kinds)
    sources = ones_where(iota((CHIPS, CHIPS), 1) < iota((CHIPS, CHIPS), 0))
    lane = iota((CHIPS, 128), 1)

    def column(values, chip):
        return jnp.sum(jnp.where(lane == chip, values, 0.0), axis=1, keepdims=True)

    for_me = dest == me
    before = ones_where(iota((LOCAL, LOCAL), 0) < iota((LOCAL, LOCAL), 1))
    rank = nn_dot(ones_where(for_me), before).astype(I32)
    over = rank - CAP
    slots = CHIPS * CAP
    spread = jnp.where(iota((CHIPS, slots), 1) // CAP == iota((CHIPS, slots), 0), 1.0, 0.0)
    along = lambda col: jnp.sum(col * spread, axis=0, keepdims=True).astype(I32)
    slot_lane = iota((1, slots), 1) % CAP
    relay = jnp.full((CHIPS, LOCAL), -1, I32)
    handed = jnp.full((1, slots), -1, I32)
    for shift in range(1, GROUP):
        amount = jnp.zeros((CHIPS, 128), F32)
        begin = amount
        base = amount
        for kind in range(CLASSES):
            for n in range(TRIES):
                if shift_of(n, kind) == shift:
                    amount = jnp.where(kinds == kind, amounts[n], amount)
                    begin = jnp.where(kinds == kind, starts[n], begin)
                    base = jnp.where(kinds == kind, bases[n], base)
        prefix = nn_dot(sources, amount.astype(BF16))
        left = left + jnp.maximum(jnp.sum(amount, axis=0, keepdims=True) - BACK, 0.0)
        order = over - column(begin, me).astype(I32)
        at = (mine + shift) % GROUP * BACK + column(prefix, me).astype(I32) + order
        relay = jnp.where((order >= 0) & (order < column(amount, me).astype(I32)), at, relay)
        near = (mine + GROUP - shift) % GROUP
        order = slot_lane - along(column(base, me))
        at = near * BACK + order + along(column(prefix, first + near))
        handed = jnp.where((order >= 0) & (order < along(column(amount, first + near))), at, handed)
    forward_ref[...] = ones_where(iota((GROUP * BACK, slots), 0) == handed)
    left_ref[0] = jnp.max(left).astype(I32)
    relay_ref[...] = jnp.where(for_me & (turn < 0), relay, -1)
    group = iota((CHIPS, LOCAL), 0) % (128 // CAP)
    later = rank - jnp.maximum(turn, 0) * CAP
    slot_ref[...] = jnp.where(for_me & (later >= 0) & (later < CAP), later + group * CAP, -1)
    here_ref[...] = jnp.where(for_me, gz * 4 + gx % 4, -1)
    down_256 = iota((LOCAL, LOCAL), 0)
    side_ref[...] = jnp.zeros((LOCAL, 128), F32)
    for part in range(slots // 128):

        def source(index, place):
            row = pl.ds(part * (128 // CAP) + index, 1)
            here = ones_where(down_256 == here_ref[row, :])
            wanted = jnp.concatenate(
                [ones_where(down_128 == slot_ref[row, :]), ones_where(down_128 == relay_ref[row, :])], axis=0
            )
            both = nt_dot(here, wanted)
            side_ref[...] += both[:, 128:]
            return place + both[:, :128]

        place = lax.fori_loop(0, 128 // CAP, source, jnp.zeros((LOCAL, 128), F32), unroll=4)
        place_ref[:, part * 128 : part * 128 + 128] = place.astype(BF16)
    relay_place_ref[...] = side_ref[...].astype(BF16)


def index_maps(pos, cell):
    vmem = pl.BlockSpec(memory_space=pltpu.VMEM)
    return pl.pallas_call(
        index_kernel,
        out_shape=(
            pltpu.HBM((LOCAL, CHIPS * CAP), BF16),
            pltpu.HBM((LOCAL, 128), BF16),
            jax.ShapeDtypeStruct((GROUP * BACK, CHIPS * CAP), BF16),
            jax.ShapeDtypeStruct((1,), I32),
            jax.ShapeDtypeStruct((1,), I32),
        ),
        in_specs=[pl.BlockSpec(memory_space=pltpu.SMEM), vmem],
        grid=(1,),
        out_specs=(
            pl.BlockSpec((LOCAL, CHIPS * CAP), lambda s: (0, 0)),
            pl.BlockSpec((LOCAL, 128), lambda s: (0, 0)),
            pl.BlockSpec((GROUP * BACK, CHIPS * CAP), lambda s: (0, 0)),
            pl.BlockSpec(memory_space=pltpu.SMEM),
            pl.BlockSpec(memory_space=pltpu.SMEM),
        ),
        scratch_shapes=[pltpu.VMEM((CHIPS, LOCAL), I32)] * 4
        + [pltpu.VMEM((CHIPS, 128), F32), pltpu.VMEM((LOCAL, 128), F32)],
        compiler_params=params(),
        cost_estimate=pl.CostEstimate(flops=10**10, bytes_accessed=10**6, transcendentals=0),
        name="index_maps",
    )(pos, cell)


def key_kernel(pos_ref, cell_ref, key_z_ref, key_x_ref, ahead_z_ref, ahead_x_ref, here_ref, there_ref):
    plane, z = pos_ref[0], pos_ref[1]
    cell = cell_ref[...]
    gx, gz, gy = cell % 64, cell // 64 % 64, cell // 4096
    here_ref[...] = jnp.where((gy == z) & (gx // 4 == plane), gz * 4 + gx % 4, -1)
    there_ref[...] = jnp.where((gy == z) & (gz // 4 == plane), gx // 4 * 16 + gz % 4 * 4 + gx % 4, -1)
    down = iota((LOCAL, LOCAL), 0)
    byte = iota((8, LOCAL), 0)

    def key_bytes(row):
        return jnp.where(
            byte == 0, row % 256, jnp.where(byte == 1, row // 256 % 256, jnp.where(byte == 2, row // 65536, 0))
        ).astype(F32).astype(BF16)

    def source(index, sums):
        row = pl.ds(index, 1)
        return (
            sums[0] + nt_dot(ones_where(down == here_ref[row, :]), key_bytes(key_z_ref[row, :])),
            sums[1] + nt_dot(ones_where(down == there_ref[row, :]), key_bytes(key_x_ref[row, :])),
        )

    nothing = jnp.zeros((LOCAL, 8), F32)
    sums = lax.fori_loop(0, CHIPS, source, (nothing, nothing), unroll=4)
    across = iota((LOCAL, LOCAL), 1)

    def key_of(part):
        return jnp.broadcast_to(part[:, 0:1] + 256.0 * part[:, 1:2] + 65536.0 * part[:, 2:3], (LOCAL, LOCAL))

    key_z, key_x = key_of(sums[0]), key_of(sums[1])
    ahead_z_ref[...] = ones_where((key_z < key_z.T) & (down % 4 == across % 4))
    ahead_x_ref[...] = ones_where((key_x.T < key_x) & (down // 4 % 4 == across // 4 % 4))


def order_keys(pos, cell, key_z, key_x):
    vmem = pl.BlockSpec(memory_space=pltpu.VMEM)
    ahead = jax.ShapeDtypeStruct((LOCAL, LOCAL), BF16)
    return pl.pallas_call(
        key_kernel,
        out_shape=(ahead, ahead),
        in_specs=[pl.BlockSpec(memory_space=pltpu.SMEM), vmem, vmem, vmem],
        out_specs=(vmem,) * 2,
        scratch_shapes=[pltpu.VMEM((CHIPS, LOCAL), I32)] * 2,
        compiler_params=params(),
        cost_estimate=pl.CostEstimate(flops=10**10, bytes_accessed=10**6, transcendentals=0),
        name="order_keys",
    )(pos, cell, key_z, key_x)


def forward_kernel(forward_ref, recv_ref, out_ref):
    out_ref[...] = nn_dot(forward_ref[...], recv_ref[...]).astype(BF16)


def forward(maps, received):
    vmem = pl.BlockSpec(memory_space=pltpu.VMEM)
    handed = pl.pallas_call(
        forward_kernel,
        out_shape=jax.ShapeDtypeStruct((GROUP * BACK, HALF), BF16),
        in_specs=[vmem, vmem],
        out_specs=vmem,
        compiler_params=params(),
        cost_estimate=pl.CostEstimate(flops=10**8, bytes_accessed=10**6, transcendentals=0),
        name="hand_on",
    )(maps, received)
    sent = lax.all_to_all(handed.reshape(GROUP, BACK, HALF), NEAR, split_axis=0, concat_axis=0, tiled=True)
    return sent.reshape(GROUP * BACK, HALF)


def unpack_kernel(place_ref, relay_ref, recv_ref, back_ref, out_ref, cells_ref, sems):
    copies = []
    for at in range(HALF // PIECE):
        lanes = pl.ds(at * PIECE, PIECE)
        cells = nn_dot(place_ref[...], recv_ref[:, lanes]) + nn_dot(relay_ref[:, : GROUP * BACK], back_ref[:, lanes])
        cells_ref[:, lanes] = cells.astype(BF16)
        copies.append(pltpu.make_async_copy(cells_ref.at[:, lanes], out_ref.at[:, lanes], sems.at[at]))
        copies[-1].start()
    for copy in copies:
        copy.wait()


def unpack(place, relay_place, received, back):
    vmem = pl.BlockSpec(memory_space=pltpu.VMEM)
    return pl.pallas_call(
        unpack_kernel,
        out_shape=pltpu.HBM((LOCAL, HALF), BF16),
        in_specs=[vmem] * 4,
        out_specs=pl.BlockSpec(memory_space=pltpu.HBM),
        scratch_shapes=[pltpu.VMEM((LOCAL, HALF), BF16), pltpu.SemaphoreType.DMA((HALF // PIECE,))],
        compiler_params=params(),
        cost_estimate=pl.CostEstimate(flops=10**9, bytes_accessed=3 * 10**6, transcendentals=0),
        name="unpack_inbox",
    )(place, relay_place, received, back)


def render_group(views, pos_ref, transfer_ref, halves, weights_ref, tile_x_ref, tile_z_ref, plane_ref, state_ref):
    with_x, with_z = "x" in views, "z" in views

    for x in range(EDGE):
        operand = jnp.concatenate([ref[:, x * 128 : x * 128 + 128] for ref in halves], axis=1)
        plane_ref[x] = nt_dot(weights_ref[pos_ref[2]], operand).reshape(32, 8, 128)
    slope = [transfer_ref[0, 0] * LOG2E] + [0.5 * transfer_ref[0, c] for c in (1, 2, 3)]
    offset = [transfer_ref[1, 0] * LOG2E] + [0.5 * transfer_ref[1, c] for c in (1, 2, 3)]
    zero = jnp.zeros((8, 128), F32)
    one = jnp.ones((8, 128), F32)
    if with_x:
        state_ref[0] = jnp.ones((32, 8, 128), F32)
        for n in range(1, 5):
            state_ref[n] = jnp.zeros((32, 8, 128), F32)

    def classify(sample):
        grown = jnp.exp2(slope[0] * sample + offset[0])
        above = 1.0 + grown
        dense = jnp.log2(above) * (grown * pl.reciprocal(above - 1.0, approx=True))
        alpha = dense * (KAPPA - dense * (KAPPA * KAPPA / 2 - dense * (KAPPA * KAPPA * KAPPA / 6)))
        return dense, alpha, [jnp.tanh(slope[c] * sample + offset[c]) for c in (1, 2, 3)]

    def advance(state, values):
        dense, alpha, colours = values
        weight = alpha * state[0]
        return (
            state[0] - weight,
            state[1] + colours[0] * weight,
            state[2] + colours[1] * weight,
            state[3] + colours[2] * weight,
            state[4] + dense,
        )

    def result(state):
        depth = KAPPA * state[4]
        half = 0.5 * opacity(depth)
        return [half + 0.5 * state[1], half + 0.5 * state[2], half + 0.5 * state[3], depth]

    def coded(state):
        depth = KAPPA * state[4]
        scale = TOP / opacity(depth)
        codes = [jnp.floor(scale * state[c] + 0.5) for c in (1, 2, 3)]
        codes.append(jnp.floor((jnp.log2(depth) - LOG_MID) * (TOP / LOG_REACH) + 0.5))
        return [jnp.clip(code, -TOP, TOP) for code in codes]

    def slab(x, carry):
        left = jnp.maximum(x - 1, 0)
        right = jnp.minimum(x + 1, EDGE - 1)

        def columns(view_even, view_odd):
            for k in range(32):
                centre = 3.0 * plane_ref[x, k]
                even = classify(centre + plane_ref[left, k])
                odd = classify(centre + plane_ref[right, k])
                if with_z:
                    view_even = advance(view_even, even)
                    view_odd = advance(view_odd, odd)
                if with_x:
                    state = tuple(state_ref[n, k] for n in range(5))
                    state = advance(advance(state, even), odd)
                    for n in range(5):
                        state_ref[n, k] = state[n]
            return view_even, view_odd

        start = (one, zero, zero, zero, zero)
        pixels = columns(start, start)
        for odd in range(2 if with_z else 0):
            values = result(pixels[odd])
            for c in range(4):
                tile_z_ref[c, 2 * x + odd] = values[c]
        return carry

    lax.fori_loop(0, EDGE, slab, 0)
    if with_x:
        values = coded([state_ref[n] for n in range(5)])
        for c in range(4):
            tile_x_ref[:, c * 256 : c * 256 + 256] = values[c].reshape(256, 128).T.astype(I32).astype(jnp.int16)


def render_kernel(views, count, kept, pos_ref, transfer_ref, *refs):
    halves, weights_ref, rest = refs[:count], refs[count], list(refs[count + 1 + kept :])
    tile_x_ref = rest.pop(0) if "x" in views else None
    tile_z_ref = rest.pop(0) if "z" in views else None
    plane_ref, state_ref = rest
    render_group(views, pos_ref, transfer_ref, halves, weights_ref, tile_x_ref, tile_z_ref, plane_ref, state_ref)


def render(views, pos, transfer, weights, *halves, before=()):
    smem = pl.BlockSpec(memory_space=pltpu.SMEM)
    batch = len(before)
    out_specs, out_shape = [], []
    if "x" in views:
        out_specs.append(pl.BlockSpec((128, 1024), lambda g: (g, batch)))
        out_shape.append(pltpu.HBM((LOCAL, 2048), jnp.int16))
    if "z" in views:
        out_specs.append(pl.BlockSpec((4, 32, 8, 128), lambda g: (0, 0, 0, g)))
        out_shape.append(pltpu.HBM((4, 32, 8, LOCAL), F32))
    return pl.pallas_call(
        functools.partial(render_kernel, views, len(halves), batch),
        grid=(2,),
        in_specs=[smem, smem]
        + [pl.BlockSpec((128, HALF), lambda g: (g, 0))] * len(halves)
        + [pl.BlockSpec(weights.shape, lambda g: (0, 0, 0))]
        + [pl.BlockSpec(memory_space=pl.ANY)] * batch,
        out_specs=out_specs,
        input_output_aliases={3 + len(halves): 0} if before else {},
        scratch_shapes=[pltpu.VMEM((EDGE, 32, 8, 128), F32), pltpu.VMEM((5, 32, 8, 128), F32)],
        out_shape=out_shape,
        compiler_params=params(semantics=("arbitrary",)),
        cost_estimate=pl.CostEstimate(flops=10**10, bytes_accessed=10**7, transcendentals=10**7),
        name="render_" + views,
    )(pos, transfer, in_hbm(halves[0]), *halves[1:], weights, *before)


def to_frame(core, sums):
    rows = iota((8, 256), 0)
    rows = jnp.where(core == 0, rows, 7 - rows)
    keep = iota((8, 256), 1) % 8 == rows
    picture = jnp.zeros((64, 128), F32)
    for tile in range(4):
        lines = []
        for c in range(4):
            for batch in range(2):
                line = jnp.where(core == 0, sums[batch][c], sums[1 - batch][c])[tile : tile + 1]
                lines.append(jnp.where(keep, line, 0.0))
        spread = ones_where(iota((256, 128), 0) // 8 + 32 * tile == iota((256, 128), 1))
        stacked = nn_dot(jnp.concatenate(parts_of(jnp.concatenate(lines, axis=0), 3), axis=0), spread)
        picture += stacked[:64] + stacked[64:128] + stacked[128:]
    return jnp.concatenate([picture[:48], opacity(picture[48:])], axis=0).reshape(4, 16, 128)


def compose_z_kernel(pos_ref, ahead_ref, first_ref, second_ref, out_ref):
    ahead = ahead_ref[...]
    group = ones_where(iota((8, LOCAL), 0) == iota((8, LOCAL), 1) % 4)
    sums = []
    for tile in (first_ref, second_ref):
        depth = tile[3].reshape(256, LOCAL)
        pieces = parts_of(depth, 3)
        through = jnp.exp(-sum(nn_dot(piece, ahead) for piece in pieces))
        values = [parts_of(tile[c].reshape(256, LOCAL) * through, 3) for c in range(3)] + [pieces]
        sums.append([sum(nt_dot(group, piece) for piece in pieces) for pieces in values])
    out_ref[...] = to_frame(pos_ref[2], sums)


FRAME = jax.ShapeDtypeStruct((4, 16, 128), F32)


def compose_z(pos, ahead, *tiles):
    return pl.pallas_call(
        compose_z_kernel,
        out_shape=FRAME,
        in_specs=[pl.BlockSpec(memory_space=pltpu.SMEM)] + [pl.BlockSpec(memory_space=pltpu.VMEM)] * 3,
        out_specs=pl.BlockSpec(memory_space=pltpu.VMEM),
        compiler_params=params(),
        cost_estimate=pl.CostEstimate(flops=10**9, bytes_accessed=4 * 10**6, transcendentals=10**5),
        name="compose_z",
    )(pos, ahead, *tiles)


def compose_x_kernel(pos_ref, ahead_ref, tile_ref, out_ref):
    ahead = ahead_ref[...]
    group = ones_where(iota((8, 48), 0) == iota((8, 48), 1) % 16 // 4)
    sums = []
    for batch in range(2):
        codes = []
        for c in range(4):
            at = batch * 1024 + c * 256
            codes.append(tile_ref[:, at : at + 256].astype(I32).astype(F32))
        depth = jnp.exp2(codes[3] * (LOG_REACH / TOP) + LOG_MID)
        through = jnp.exp(-sum(nn_dot(ahead, piece) for piece in parts_of(depth, 3)))
        scale = (0.5 * opacity(depth)) * through
        values = [scale + scale * (codes[c] * (1.0 / TOP)) for c in range(3)] + [depth]
        folded = [jnp.sum(value.reshape(16, 16, 256), axis=0) for value in values]
        sums.append([nn_dot(group, jnp.concatenate(parts_of(fold, 3), axis=0)) for fold in folded])
    out_ref[...] = to_frame(pos_ref[2], sums)


def compose_x(pos, ahead, tiles):
    return pl.pallas_call(
        compose_x_kernel,
        out_shape=FRAME,
        in_specs=[pl.BlockSpec(memory_space=pltpu.SMEM)] + [pl.BlockSpec(memory_space=pltpu.VMEM)] * 2,
        out_specs=pl.BlockSpec(memory_space=pltpu.VMEM),
        compiler_params=params(),
        cost_estimate=pl.CostEstimate(flops=10**9, bytes_accessed=10**6, transcendentals=10**5),
        name="compose_x",
    )(pos, ahead, tiles)


def swap_cores(values):
    return lax.ppermute(values, "c", [(0, 1), (1, 0)])


def send_bricks(outbox):
    lanes = outbox.shape[1]
    sent = lax.all_to_all(outbox.reshape(CHIPS, CAP, lanes), CHIP, split_axis=0, concat_axis=0, tiled=True)
    return sent.reshape(CHIPS * CAP, lanes)


def send_tiles(tiles):
    sent = lax.all_to_all(tiles.reshape(16, 16, 2048), PLANE, split_axis=0, concat_axis=0, tiled=True)
    return sent.reshape(LOCAL, 2048)


def body(bricks, transfer, assignment, brick_cell, depth_rank):
    plane = lax.axis_index(PLANE)
    z = lax.axis_index("z")
    core = lax.axis_index("c")
    chip = plane * 4 + z

    def position(turn):
        return jnp.stack([plane, z, core, turn]).astype(I32)

    start = position(jnp.int32(-1))
    cell_row = lax.dynamic_slice_in_dim(brick_cell, chip * LOCAL, LOCAL).reshape(1, LOCAL)
    weights = [plane_weights(0), plane_weights(1)]
    other = swap_cores(bricks)

    outbox = pack(start, plan_slots(start, cell_row), bricks, other)
    outbox, brick_cell, assignment, depth_rank = lax.optimization_barrier((outbox, brick_cell, assignment, depth_rank))
    inbox = send_bricks(outbox)
    cell = brick_cell.reshape(CHIPS, LOCAL)
    major = assignment.reshape(CHIPS, LOCAL) * 16384
    key_z = major + depth_rank[0].reshape(CHIPS, LOCAL)
    key_x = major + depth_rank[1].reshape(CHIPS, LOCAL)
    place, relay_place, handing, most, left = index_maps(start, cell)
    keys = order_keys(start, cell, key_z, key_x)
    handing, keys = lax.optimization_barrier((handing, keys))
    cells = unpack(place, relay_place, inbox, forward(handing, inbox))

    def frames_of(cells):
        other_half = swap_cores(cells)
        tile_x, first_z = render("xz", start, transfer, weights[0], cells)
        (tile_x,) = render("x", start, transfer, weights[1], cells, other_half, before=(tile_x,))
        cells, tile_x = lax.optimization_barrier((cells, tile_x))
        landed = send_tiles(tile_x)
        (later_z,) = render("z", start, transfer, weights[1], cells, other_half)
        ahead_z, ahead_x = keys
        return compose_z(start, ahead_z, first_z, later_z), compose_x(start, ahead_x, landed)

    def in_rounds(carry):
        rounds = (most.reshape(()) + CAP - 1) // CAP

        def next_round(carry):
            turn, cells = carry
            pos = position(turn)
            place = index_maps(pos, cell)[0]
            inbox = send_bricks(pack(pos, plan_slots(pos, cell_row), bricks, other))
            return turn + 1, cells + unpack(place, relay_place, inbox, jnp.zeros((GROUP * BACK, HALF), BF16))

        nothing = (jnp.int32(0), jnp.zeros((LOCAL, HALF), BF16))
        _, cells = lax.while_loop(lambda carry: carry[0] < rounds, next_round, nothing)
        return (jnp.zeros_like(carry[0]),) + frames_of(cells)

    carry = (left.reshape(()),) + frames_of(cells)
    return lax.while_loop(lambda carry: carry[0] > 0, in_rounds, carry)[1:]


def solution(mesh):
    fine = Mesh(mesh.devices.reshape(4, 2, 2, 4, 2), CHIP + ("c",))
    in_specs = (P(CHIP + ("c",), None), P(), P(), P(), P())
    out_specs = (P(None, ("z", "c"), PLANE), P(None, ("z", "c"), PLANE))
    return jax.shard_map(body, mesh=fine, in_specs=in_specs, out_specs=out_specs, check_vma=False)
```

```python
import functools

import jax
import jax.numpy as jnp
import numpy as np
from jax import lax
from jax.experimental import pallas as pl
from jax.experimental.pallas import tpu as pltpu
from jax.sharding import Mesh
from jax.sharding import PartitionSpec as P

SIDE = 1024
EDGE = 16
CAP = 8
TRIES = 5
GROUP = 8
CLASSES = 4
BACK = 8
CHIPS = 64
LOCAL = 256
HALF = EDGE * EDGE * EDGE // 2
PIECE = 512
F32 = jnp.float32
BF16 = jnp.bfloat16
I32 = jnp.int32
LOG2E = 1.4426950408889634
KAPPA = 2.0 * 0.6931471805599453 / SIDE
PLANE = ("y", "x1", "x0")
CHIP = ("y", "x1", "x0", "z")
NEAR = ("x0", "z")


TOP = 32767.0
LOG_MID = -9.88
LOG_REACH = 9.3


def iota(shape, axis):
    return lax.broadcasted_iota(I32, shape, axis)


def ones_where(mask):
    return jnp.where(mask, 1.0, 0.0).astype(BF16)


def nt_dot(left, right):
    return lax.dot_general(left, right, (((1,), (1,)), ((), ())), preferred_element_type=F32)


def nn_dot(left, right):
    return jnp.dot(left, right, preferred_element_type=F32)


def opacity(depth):
    half = jnp.tanh(0.5 * depth)
    return 2.0 * half / (1.0 + half)


def parts_of(values, count):
    pieces = []
    rest = values
    for _ in range(count - 1):
        piece = rest.astype(BF16)
        pieces.append(piece)
        rest = rest - piece.astype(F32)
    return pieces + [rest.astype(BF16)]


def in_hbm(array):
    return pltpu.with_memory_space_constraint(array, pltpu.HBM)


def params(mib=24, semantics=None):
    return pltpu.CompilerParams(vmem_limit_bytes=mib * 1024 * 1024, dimension_semantics=semantics)


def upsample_np():
    matrix = np.zeros((2 * EDGE, EDGE), np.float32)
    for row in range(2 * EDGE):
        centre = row // 2
        beside = min(max(centre - 1 if row % 2 == 0 else centre + 1, 0), EDGE - 1)
        matrix[row, centre] += 0.75
        matrix[row, beside] += 0.25
    return matrix


def plane_weights(batch):
    up = upsample_np()
    out = np.zeros((2, 32, 8, 1 + batch, 8, 16), np.float32)
    for core in range(2):
        for sub in range(8):
            centre = 4 * batch + sub // 2
            beside = max(centre - 1, 0) if sub % 2 == 0 else centre + 1
            for m, share in ((centre, 0.75), (beside, 0.25)):
                half, y = m // 8, m % 8
                out[core, :, sub, half, y if core == 0 else 7 - y] += 0.25 * share * up
    return jnp.asarray(out.reshape(2, 256, 128 * (1 + batch)), BF16)


def chip_of(cell):
    return (cell % 64) // 4 * 4 + cell // 4096


def up(values, shift):
    inside = iota(values.shape, 1) % GROUP + shift < GROUP
    return jnp.where(inside, pltpu.roll(values, 128 - shift, axis=1), pltpu.roll(values, GROUP - shift, axis=1))


def shift_of(turn, kind):
    return 1 + (turn + 2 * kind) % (GROUP - 1)


def by_class(values, kinds, turn, back):
    out = None
    for kind in range(CLASSES):
        shift = shift_of(turn, kind)
        moved = up(values, GROUP - shift if back else shift)
        out = moved if out is None else jnp.where(kinds == kind, moved, out)
    return out


def relay_plan(counts, kinds):
    over = jnp.maximum(counts - CAP, 0.0)
    taken = jnp.minimum(counts, CAP)
    begin = jnp.zeros_like(over)
    amounts, starts, bases = [], [begin], []
    for turn in range(TRIES):
        amount = jnp.minimum(over, CAP - by_class(taken, kinds, turn, False))
        bases.append(taken)
        taken = taken + by_class(amount, kinds, turn, True)
        over = over - amount
        begin = begin + amount
        amounts.append(amount)
        starts.append(begin)
    return amounts, starts, bases, over


def plan_kernel(pos_ref, cell_ref, slot_ref):
    turn = pos_ref[3]
    kind = (pos_ref[0] * 4 + pos_ref[1]) % CLASSES
    dest = chip_of(cell_ref[...])
    across = jnp.broadcast_to(dest, (LOCAL, LOCAL))
    down = across.astype(F32).T.astype(I32)
    earlier = (down == across) & (iota((LOCAL, LOCAL), 0) < iota((LOCAL, LOCAL), 1))
    rank = jnp.sum(earlier.astype(I32), axis=0, keepdims=True)
    later = rank - turn * CAP
    in_turn = jnp.where((later >= 0) & (later < CAP), dest * CAP + later, -1)
    chips = iota((128, LOCAL), 0)
    counts = nt_dot(jnp.ones((8, LOCAL), BF16), ones_where(chips % CHIPS == dest))
    kinds = jnp.full((8, 128), kind, I32)
    _, starts, bases, _ = relay_plan(counts, kinds)
    rows = starts[1:] + [by_class(base, kinds, n, False) for n, base in enumerate(bases)]
    table = jnp.concatenate([row[0:1] for row in rows] + [jnp.zeros((16 - len(rows), 128), F32)], axis=0)
    found = nn_dot(table.astype(BF16), ones_where(chips == dest)).astype(I32)
    relayed = jnp.where(rank < CAP, dest * CAP + rank, -1)
    over = rank - CAP
    for n in range(TRIES):
        begin = found[n - 1 : n] if n else jnp.zeros_like(over)
        inside = (over >= begin) & (over < found[n : n + 1])
        relay = dest // GROUP * GROUP + (dest + shift_of(n, kind)) % GROUP
        relayed = jnp.where(inside, relay * CAP + found[TRIES + n : TRIES + n + 1] + over - begin, relayed)
    slot_ref[...] = jnp.where(turn < 0, relayed, in_turn)


def plan_slots(pos, cell_row):
    return pl.pallas_call(
        plan_kernel,
        out_shape=jax.ShapeDtypeStruct((1, LOCAL), I32),
        in_specs=[pl.BlockSpec(memory_space=pltpu.SMEM), pl.BlockSpec(memory_space=pltpu.VMEM)],
        out_specs=pl.BlockSpec(memory_space=pltpu.VMEM),
        compiler_params=params(),
        cost_estimate=pl.CostEstimate(flops=10**9, bytes_accessed=10**6, transcendentals=0),
        name="plan_slots",
    )(pos, cell_row)


def pack_kernel(pos_ref, slot_ref, bricks_ref, other_ref, out_ref, full_ref, box_ref, sems):
    core = pos_ref[2]
    slot = slot_ref[...]
    for n, ref in enumerate((bricks_ref, other_ref)):
        rows = pl.ds(pl.multiple_of((core + n) % 2 * 128, 128), 128)
        for x in range(EDGE):
            start = pl.multiple_of(x * 256 + core * 128, 128)
            full_ref[rows, x * 128 : x * 128 + 128] = ref[:, pl.ds(start, 128)]
    pick = ones_where(iota((CHIPS * CAP, LOCAL), 0) == slot)
    copies = []
    for at in range(HALF // PIECE):
        lanes = pl.ds(at * PIECE, PIECE)
        box_ref[:, lanes] = nn_dot(pick, full_ref[:, lanes]).astype(BF16)
        copy = pltpu.make_async_copy(box_ref.at[:, lanes], out_ref.at[:, lanes], sems.at[at])
        copy.start()
        copies.append(copy)
    for copy in copies:
        copy.wait()


def pack(pos, slot, bricks, other):
    rows = CHIPS * CAP
    return pl.pallas_call(
        pack_kernel,
        in_specs=[pl.BlockSpec(memory_space=pltpu.SMEM)] + [pl.BlockSpec(memory_space=pltpu.VMEM)] * 3,
        out_specs=pl.BlockSpec(memory_space=pltpu.HBM),
        scratch_shapes=[
            pltpu.VMEM((LOCAL, HALF), BF16),
            pltpu.VMEM((rows, HALF), BF16),
            pltpu.SemaphoreType.DMA((HALF // PIECE,)),
        ],
        out_shape=pltpu.HBM((rows, HALF), BF16),
        compiler_params=params(),
        name="pack_outbox",
    )(pos, slot, bricks, other)


def index_kernel(
    pos_ref, cell_ref, place_ref, relay_place_ref, forward_ref, most_ref, left_ref,
    here_ref, slot_ref, relay_ref, dest_ref, count_ref, side_ref
):
    plane, z, turn = pos_ref[0], pos_ref[1], pos_ref[3]
    me = plane * 4 + z
    mine = me % GROUP
    first = me - mine
    cell = cell_ref[...]
    gx, gz = cell % 64, cell // 64 % 64
    dest = chip_of(cell)
    dest_ref[...] = dest
    down_128 = iota((128, LOCAL), 0)
    down_chip = down_128 % CHIPS
    units = jnp.ones((8, LOCAL), BF16)

    def count(index, carry):
        row = pl.ds(index, 1)
        count_ref[row, :] = nt_dot(units, ones_where(down_chip == dest_ref[row, :]))[0:1]
        return carry

    lax.fori_loop(0, CHIPS, count, 0, unroll=8)
    counts = count_ref[...]
    most_ref[0] = jnp.max(counts).astype(I32)
    kinds = iota((CHIPS, 128), 0) % CLASSES
    amounts, starts, bases, left = relay_plan(counts, kinds)
    sources = ones_where(iota((CHIPS, CHIPS), 1) < iota((CHIPS, CHIPS), 0))
    lane = iota((CHIPS, 128), 1)

    def column(values, chip):
        return jnp.sum(jnp.where(lane == chip, values, 0.0), axis=1, keepdims=True)

    for_me = dest == me
    before = ones_where(iota((LOCAL, LOCAL), 0) < iota((LOCAL, LOCAL), 1))
    rank = nn_dot(ones_where(for_me), before).astype(I32)
    over = rank - CAP
    slots = CHIPS * CAP
    spread = jnp.where(iota((CHIPS, slots), 1) // CAP == iota((CHIPS, slots), 0), 1.0, 0.0)
    along = lambda col: jnp.sum(col * spread, axis=0, keepdims=True).astype(I32)
    slot_lane = iota((1, slots), 1) % CAP
    relay = jnp.full((CHIPS, LOCAL), -1, I32)
    handed = jnp.full((1, slots), -1, I32)
    for shift in range(1, GROUP):
        amount = jnp.zeros((CHIPS, 128), F32)
        begin = amount
        base = amount
        for kind in range(CLASSES):
            for n in range(TRIES):
                if shift_of(n, kind) == shift:
                    amount = jnp.where(kinds == kind, amounts[n], amount)
                    begin = jnp.where(kinds == kind, starts[n], begin)
                    base = jnp.where(kinds == kind, bases[n], base)
        prefix = nn_dot(sources, amount.astype(BF16))
        left = left + jnp.maximum(jnp.sum(amount, axis=0, keepdims=True) - BACK, 0.0)
        order = over - column(begin, me).astype(I32)
        at = (mine + shift) % GROUP * BACK + column(prefix, me).astype(I32) + order
        relay = jnp.where((order >= 0) & (order < column(amount, me).astype(I32)), at, relay)
        near = (mine + GROUP - shift) % GROUP
        order = slot_lane - along(column(base, me))
        at = near * BACK + order + along(column(prefix, first + near))
        handed = jnp.where((order >= 0) & (order < along(column(amount, first + near))), at, handed)
    forward_ref[...] = ones_where(iota((GROUP * BACK, slots), 0) == handed)
    left_ref[0] = jnp.max(left).astype(I32)
    relay_ref[...] = jnp.where(for_me & (turn < 0), relay, -1)
    group = iota((CHIPS, LOCAL), 0) % (128 // CAP)
    later = rank - jnp.maximum(turn, 0) * CAP
    slot_ref[...] = jnp.where(for_me & (later >= 0) & (later < CAP), later + group * CAP, -1)
    here_ref[...] = jnp.where(for_me, gz * 4 + gx % 4, -1)
    down_256 = iota((LOCAL, LOCAL), 0)
    side_ref[...] = jnp.zeros((LOCAL, 128), F32)
    for part in range(slots // 128):

        def source(index, place):
            row = pl.ds(part * (128 // CAP) + index, 1)
            here = ones_where(down_256 == here_ref[row, :])
            wanted = jnp.concatenate(
                [ones_where(down_128 == slot_ref[row, :]), ones_where(down_128 == relay_ref[row, :])], axis=0
            )
            both = nt_dot(here, wanted)
            side_ref[...] += both[:, 128:]
            return place + both[:, :128]

        place = lax.fori_loop(0, 128 // CAP, source, jnp.zeros((LOCAL, 128), F32), unroll=4)
        place_ref[:, part * 128 : part * 128 + 128] = place.astype(BF16)
    relay_place_ref[...] = side_ref[...].astype(BF16)


def index_maps(pos, cell):
    vmem = pl.BlockSpec(memory_space=pltpu.VMEM)
    return pl.pallas_call(
        index_kernel,
        out_shape=(
            pltpu.HBM((LOCAL, CHIPS * CAP), BF16),
            pltpu.HBM((LOCAL, 128), BF16),
            jax.ShapeDtypeStruct((GROUP * BACK, CHIPS * CAP), BF16),
            jax.ShapeDtypeStruct((1,), I32),
            jax.ShapeDtypeStruct((1,), I32),
        ),
        in_specs=[pl.BlockSpec(memory_space=pltpu.SMEM), vmem],
        grid=(1,),
        out_specs=(
            pl.BlockSpec((LOCAL, CHIPS * CAP), lambda s: (0, 0)),
            pl.BlockSpec((LOCAL, 128), lambda s: (0, 0)),
            pl.BlockSpec((GROUP * BACK, CHIPS * CAP), lambda s: (0, 0)),
            pl.BlockSpec(memory_space=pltpu.SMEM),
            pl.BlockSpec(memory_space=pltpu.SMEM),
        ),
        scratch_shapes=[pltpu.VMEM((CHIPS, LOCAL), I32)] * 4
        + [pltpu.VMEM((CHIPS, 128), F32), pltpu.VMEM((LOCAL, 128), F32)],
        compiler_params=params(),
        cost_estimate=pl.CostEstimate(flops=10**10, bytes_accessed=10**6, transcendentals=0),
        name="index_maps",
    )(pos, cell)


def key_kernel(pos_ref, cell_ref, key_z_ref, key_x_ref, ahead_z_ref, ahead_x_ref, here_ref, there_ref):
    plane, z = pos_ref[0], pos_ref[1]
    cell = cell_ref[...]
    gx, gz, gy = cell % 64, cell // 64 % 64, cell // 4096
    here_ref[...] = jnp.where((gy == z) & (gx // 4 == plane), gz * 4 + gx % 4, -1)
    there_ref[...] = jnp.where((gy == z) & (gz // 4 == plane), gx // 4 * 16 + gz % 4 * 4 + gx % 4, -1)
    down = iota((LOCAL, LOCAL), 0)
    byte = iota((8, LOCAL), 0)

    def key_bytes(row):
        return jnp.where(
            byte == 0, row % 256, jnp.where(byte == 1, row // 256 % 256, jnp.where(byte == 2, row // 65536, 0))
        ).astype(F32).astype(BF16)

    def source(index, sums):
        row = pl.ds(index, 1)
        return (
            sums[0] + nt_dot(ones_where(down == here_ref[row, :]), key_bytes(key_z_ref[row, :])),
            sums[1] + nt_dot(ones_where(down == there_ref[row, :]), key_bytes(key_x_ref[row, :])),
        )

    nothing = jnp.zeros((LOCAL, 8), F32)
    sums = lax.fori_loop(0, CHIPS, source, (nothing, nothing), unroll=4)
    across = iota((LOCAL, LOCAL), 1)

    def key_of(part):
        return jnp.broadcast_to(part[:, 0:1] + 256.0 * part[:, 1:2] + 65536.0 * part[:, 2:3], (LOCAL, LOCAL))

    key_z, key_x = key_of(sums[0]), key_of(sums[1])
    ahead_z_ref[...] = ones_where((key_z < key_z.T) & (down % 4 == across % 4))
    ahead_x_ref[...] = ones_where((key_x.T < key_x) & (down // 4 % 4 == across // 4 % 4))


def order_keys(pos, cell, key_z, key_x):
    vmem = pl.BlockSpec(memory_space=pltpu.VMEM)
    ahead = jax.ShapeDtypeStruct((LOCAL, LOCAL), BF16)
    return pl.pallas_call(
        key_kernel,
        out_shape=(ahead, ahead),
        in_specs=[pl.BlockSpec(memory_space=pltpu.SMEM), vmem, vmem, vmem],
        out_specs=(vmem,) * 2,
        scratch_shapes=[pltpu.VMEM((CHIPS, LOCAL), I32)] * 2,
        compiler_params=params(),
        cost_estimate=pl.CostEstimate(flops=10**10, bytes_accessed=10**6, transcendentals=0),
        name="order_keys",
    )(pos, cell, key_z, key_x)


def forward_kernel(forward_ref, recv_ref, out_ref):
    out_ref[...] = nn_dot(forward_ref[...], recv_ref[...]).astype(BF16)


def forward(maps, received):
    vmem = pl.BlockSpec(memory_space=pltpu.VMEM)
    handed = pl.pallas_call(
        forward_kernel,
        out_shape=jax.ShapeDtypeStruct((GROUP * BACK, HALF), BF16),
        in_specs=[vmem, vmem],
        out_specs=vmem,
        compiler_params=params(),
        cost_estimate=pl.CostEstimate(flops=10**8, bytes_accessed=10**6, transcendentals=0),
        name="hand_on",
    )(maps, received)
    sent = lax.all_to_all(handed.reshape(GROUP, BACK, HALF), NEAR, split_axis=0, concat_axis=0, tiled=True)
    return sent.reshape(GROUP * BACK, HALF)


def unpack_kernel(place_ref, relay_ref, recv_ref, back_ref, out_ref, cells_ref, sems):
    copies = []
    for at in range(HALF // PIECE):
        lanes = pl.ds(at * PIECE, PIECE)
        cells = nn_dot(place_ref[...], recv_ref[:, lanes]) + nn_dot(relay_ref[:, : GROUP * BACK], back_ref[:, lanes])
        cells_ref[:, lanes] = cells.astype(BF16)
        copies.append(pltpu.make_async_copy(cells_ref.at[:, lanes], out_ref.at[:, lanes], sems.at[at]))
        copies[-1].start()
    for copy in copies:
        copy.wait()


def unpack(place, relay_place, received, back):
    vmem = pl.BlockSpec(memory_space=pltpu.VMEM)
    return pl.pallas_call(
        unpack_kernel,
        out_shape=pltpu.HBM((LOCAL, HALF), BF16),
        in_specs=[vmem] * 4,
        out_specs=pl.BlockSpec(memory_space=pltpu.HBM),
        scratch_shapes=[pltpu.VMEM((LOCAL, HALF), BF16), pltpu.SemaphoreType.DMA((HALF // PIECE,))],
        compiler_params=params(),
        cost_estimate=pl.CostEstimate(flops=10**9, bytes_accessed=3 * 10**6, transcendentals=0),
        name="unpack_inbox",
    )(place, relay_place, received, back)


def render_group(views, pos_ref, transfer_ref, halves, weights_ref, tile_x_ref, tile_z_ref, plane_ref, state_ref):
    with_x, with_z = "x" in views, "z" in views

    for x in range(EDGE):
        operand = jnp.concatenate([ref[:, x * 128 : x * 128 + 128] for ref in halves], axis=1)
        plane_ref[x] = nt_dot(weights_ref[pos_ref[2]], operand).reshape(32, 8, 128)
    slope = [transfer_ref[0, 0] * LOG2E] + [0.5 * transfer_ref[0, c] for c in (1, 2, 3)]
    offset = [transfer_ref[1, 0] * LOG2E] + [0.5 * transfer_ref[1, c] for c in (1, 2, 3)]
    zero = jnp.zeros((8, 128), F32)
    one = jnp.ones((8, 128), F32)
    if with_x:
        state_ref[0] = jnp.ones((32, 8, 128), F32)
        for n in range(1, 5):
            state_ref[n] = jnp.zeros((32, 8, 128), F32)

    def classify(sample):
        grown = jnp.exp2(slope[0] * sample + offset[0])
        above = 1.0 + grown
        dense = jnp.log2(above) * (grown * pl.reciprocal(above - 1.0, approx=True))
        alpha = dense * (KAPPA - dense * (KAPPA * KAPPA / 2 - dense * (KAPPA * KAPPA * KAPPA / 6)))
        return dense, alpha, [jnp.tanh(slope[c] * sample + offset[c]) for c in (1, 2, 3)]

    def advance(state, values):
        dense, alpha, colours = values
        weight = alpha * state[0]
        return (
            state[0] - weight,
            state[1] + colours[0] * weight,
            state[2] + colours[1] * weight,
            state[3] + colours[2] * weight,
            state[4] + dense,
        )

    def result(state):
        depth = KAPPA * state[4]
        half = 0.5 * opacity(depth)
        return [half + 0.5 * state[1], half + 0.5 * state[2], half + 0.5 * state[3], depth]

    def coded(state):
        depth = KAPPA * state[4]
        scale = TOP / opacity(depth)
        codes = [jnp.floor(scale * state[c] + 0.5) for c in (1, 2, 3)]
        codes.append(jnp.floor((jnp.log2(depth) - LOG_MID) * (TOP / LOG_REACH) + 0.5))
        return [jnp.clip(code, -TOP, TOP) for code in codes]

    def slab(x, carry):
        left = jnp.maximum(x - 1, 0)
        right = jnp.minimum(x + 1, EDGE - 1)

        def columns(view_even, view_odd):
            for k in range(32):
                centre = 3.0 * plane_ref[x, k]
                even = classify(centre + plane_ref[left, k])
                odd = classify(centre + plane_ref[right, k])
                if with_z:
                    view_even = advance(view_even, even)
                    view_odd = advance(view_odd, odd)
                if with_x:
                    state = tuple(state_ref[n, k] for n in range(5))
                    state = advance(advance(state, even), odd)
                    for n in range(5):
                        state_ref[n, k] = state[n]
            return view_even, view_odd

        start = (one, zero, zero, zero, zero)
        pixels = columns(start, start)
        for odd in range(2 if with_z else 0):
            values = result(pixels[odd])
            for c in range(4):
                tile_z_ref[c, 2 * x + odd] = values[c]
        return carry

    lax.fori_loop(0, EDGE, slab, 0)
    if with_x:
        values = coded([state_ref[n] for n in range(5)])
        for c in range(4):
            tile_x_ref[:, c * 256 : c * 256 + 256] = values[c].reshape(256, 128).T.astype(I32).astype(jnp.int16)


def render_kernel(views, count, kept, pos_ref, transfer_ref, *refs):
    halves, weights_ref, rest = refs[:count], refs[count], list(refs[count + 1 + kept :])
    tile_x_ref = rest.pop(0) if "x" in views else None
    tile_z_ref = rest.pop(0) if "z" in views else None
    plane_ref, state_ref = rest
    render_group(views, pos_ref, transfer_ref, halves, weights_ref, tile_x_ref, tile_z_ref, plane_ref, state_ref)


def render(views, pos, transfer, weights, *halves, before=()):
    smem = pl.BlockSpec(memory_space=pltpu.SMEM)
    batch = len(before)
    out_specs, out_shape = [], []
    if "x" in views:
        out_specs.append(pl.BlockSpec((128, 1024), lambda g: (g, batch)))
        out_shape.append(pltpu.HBM((LOCAL, 2048), jnp.int16))
    if "z" in views:
        out_specs.append(pl.BlockSpec((4, 32, 8, 128), lambda g: (0, 0, 0, g)))
        out_shape.append(pltpu.HBM((4, 32, 8, LOCAL), F32))
    return pl.pallas_call(
        functools.partial(render_kernel, views, len(halves), batch),
        grid=(2,),
        in_specs=[smem, smem]
        + [pl.BlockSpec((128, HALF), lambda g: (g, 0))] * len(halves)
        + [pl.BlockSpec(weights.shape, lambda g: (0, 0, 0))]
        + [pl.BlockSpec(memory_space=pl.ANY)] * batch,
        out_specs=out_specs,
        input_output_aliases={3 + len(halves): 0} if before else {},
        scratch_shapes=[pltpu.VMEM((EDGE, 32, 8, 128), F32), pltpu.VMEM((5, 32, 8, 128), F32)],
        out_shape=out_shape,
        compiler_params=params(semantics=("arbitrary",)),
        cost_estimate=pl.CostEstimate(flops=10**10, bytes_accessed=10**7, transcendentals=10**7),
        name="render_" + views,
    )(pos, transfer, in_hbm(halves[0]), *halves[1:], weights, *before)


def to_frame(core, sums):
    rows = iota((8, 256), 0)
    rows = jnp.where(core == 0, rows, 7 - rows)
    keep = iota((8, 256), 1) % 8 == rows
    picture = jnp.zeros((64, 128), F32)
    for tile in range(4):
        lines = []
        for c in range(4):
            for batch in range(2):
                line = jnp.where(core == 0, sums[batch][c], sums[1 - batch][c])[tile : tile + 1]
                lines.append(jnp.where(keep, line, 0.0))
        spread = ones_where(iota((256, 128), 0) // 8 + 32 * tile == iota((256, 128), 1))
        stacked = nn_dot(jnp.concatenate(parts_of(jnp.concatenate(lines, axis=0), 2), axis=0), spread)
        picture += stacked[:64] + stacked[64:]
    return jnp.concatenate([picture[:48], opacity(picture[48:])], axis=0).reshape(4, 16, 128)


def compose_z_kernel(pos_ref, ahead_ref, first_ref, second_ref, out_ref):
    ahead = ahead_ref[...]
    group = ones_where(iota((8, LOCAL), 0) == iota((8, LOCAL), 1) % 4)
    sums = []
    for tile in (first_ref, second_ref):
        depth = tile[3].reshape(256, LOCAL)
        pieces = parts_of(depth, 2)
        through = jnp.exp(-sum(nn_dot(piece, ahead) for piece in pieces))
        values = [parts_of(tile[c].reshape(256, LOCAL) * through, 2) for c in range(3)] + [pieces]
        sums.append([sum(nt_dot(group, piece) for piece in pieces) for pieces in values])
    out_ref[...] = to_frame(pos_ref[2], sums)


FRAME = jax.ShapeDtypeStruct((4, 16, 128), F32)


def compose_z(pos, ahead, *tiles):
    return pl.pallas_call(
        compose_z_kernel,
        out_shape=FRAME,
        in_specs=[pl.BlockSpec(memory_space=pltpu.SMEM)] + [pl.BlockSpec(memory_space=pltpu.VMEM)] * 3,
        out_specs=pl.BlockSpec(memory_space=pltpu.VMEM),
        compiler_params=params(),
        cost_estimate=pl.CostEstimate(flops=10**9, bytes_accessed=4 * 10**6, transcendentals=10**5),
        name="compose_z",
    )(pos, ahead, *tiles)


def compose_x_kernel(pos_ref, ahead_ref, tile_ref, out_ref):
    ahead = ahead_ref[...]
    group = ones_where(iota((8, 32), 0) == iota((8, 32), 1) % 16 // 4)
    sums = []
    for batch in range(2):
        codes = []
        for c in range(4):
            at = batch * 1024 + c * 256
            codes.append(tile_ref[:, at : at + 256].astype(I32).astype(F32))
        depth = jnp.exp2(codes[3] * (LOG_REACH / TOP) + LOG_MID)
        through = jnp.exp(-sum(nn_dot(ahead, piece) for piece in parts_of(depth, 2)))
        scale = (0.5 * opacity(depth)) * through
        values = [scale + scale * (codes[c] * (1.0 / TOP)) for c in range(3)] + [depth]
        folded = [jnp.sum(value.reshape(16, 16, 256), axis=0) for value in values]
        sums.append([nn_dot(group, jnp.concatenate(parts_of(fold, 2), axis=0)) for fold in folded])
    out_ref[...] = to_frame(pos_ref[2], sums)


def compose_x(pos, ahead, tiles):
    return pl.pallas_call(
        compose_x_kernel,
        out_shape=FRAME,
        in_specs=[pl.BlockSpec(memory_space=pltpu.SMEM)] + [pl.BlockSpec(memory_space=pltpu.VMEM)] * 2,
        out_specs=pl.BlockSpec(memory_space=pltpu.VMEM),
        compiler_params=params(),
        cost_estimate=pl.CostEstimate(flops=10**9, bytes_accessed=10**6, transcendentals=10**5),
        name="compose_x",
    )(pos, ahead, tiles)


def swap_cores(values):
    return lax.ppermute(values, "c", [(0, 1), (1, 0)])


def send_bricks(outbox):
    lanes = outbox.shape[1]
    sent = lax.all_to_all(outbox.reshape(CHIPS, CAP, lanes), CHIP, split_axis=0, concat_axis=0, tiled=True)
    return sent.reshape(CHIPS * CAP, lanes)


def send_tiles(tiles):
    sent = lax.all_to_all(tiles.reshape(16, 16, 2048), PLANE, split_axis=0, concat_axis=0, tiled=True)
    return sent.reshape(LOCAL, 2048)


def body(bricks, transfer, assignment, brick_cell, depth_rank):
    plane = lax.axis_index(PLANE)
    z = lax.axis_index("z")
    core = lax.axis_index("c")
    chip = plane * 4 + z

    def position(turn):
        return jnp.stack([plane, z, core, turn]).astype(I32)

    start = position(jnp.int32(-1))
    cell_row = lax.dynamic_slice_in_dim(brick_cell, chip * LOCAL, LOCAL).reshape(1, LOCAL)
    weights = [plane_weights(0), plane_weights(1)]
    other = swap_cores(bricks)

    outbox = pack(start, plan_slots(start, cell_row), bricks, other)
    outbox, brick_cell, assignment, depth_rank = lax.optimization_barrier((outbox, brick_cell, assignment, depth_rank))
    inbox = send_bricks(outbox)
    cell = brick_cell.reshape(CHIPS, LOCAL)
    major = assignment.reshape(CHIPS, LOCAL) * 16384
    key_z = major + depth_rank[0].reshape(CHIPS, LOCAL)
    key_x = major + depth_rank[1].reshape(CHIPS, LOCAL)
    place, relay_place, handing, most, left = index_maps(start, cell)
    keys = order_keys(start, cell, key_z, key_x)
    handing, keys = lax.optimization_barrier((handing, keys))
    cells = unpack(place, relay_place, inbox, forward(handing, inbox))

    def frames_of(cells):
        other_half = swap_cores(cells)
        tile_x, first_z = render("xz", start, transfer, weights[0], cells)
        (tile_x,) = render("x", start, transfer, weights[1], cells, other_half, before=(tile_x,))
        cells, tile_x = lax.optimization_barrier((cells, tile_x))
        landed = send_tiles(tile_x)
        (later_z,) = render("z", start, transfer, weights[1], cells, other_half)
        ahead_z, ahead_x = keys
        return compose_z(start, ahead_z, first_z, later_z), compose_x(start, ahead_x, landed)

    def in_rounds(carry):
        rounds = (most.reshape(()) + CAP - 1) // CAP

        def next_round(carry):
            turn, cells = carry
            pos = position(turn)
            place = index_maps(pos, cell)[0]
            inbox = send_bricks(pack(pos, plan_slots(pos, cell_row), bricks, other))
            return turn + 1, cells + unpack(place, relay_place, inbox, jnp.zeros((GROUP * BACK, HALF), BF16))

        nothing = (jnp.int32(0), jnp.zeros((LOCAL, HALF), BF16))
        _, cells = lax.while_loop(lambda carry: carry[0] < rounds, next_round, nothing)
        return (jnp.zeros_like(carry[0]),) + frames_of(cells)

    carry = (left.reshape(()),) + frames_of(cells)
    return lax.while_loop(lambda carry: carry[0] > 0, in_rounds, carry)[1:]


def solution(mesh):
    fine = Mesh(mesh.devices.reshape(4, 2, 2, 4, 2), CHIP + ("c",))
    in_specs = (P(CHIP + ("c",), None), P(), P(), P(), P())
    out_specs = (P(None, ("z", "c"), PLANE), P(None, ("z", "c"), PLANE))
    return jax.shard_map(body, mesh=fine, in_specs=in_specs, out_specs=out_specs, check_vma=False)
```
